32 devices in a mesh: lon: 8 (over y, x, core), lat: 4 (over z).
Axes of the slice: x: 2, y: 2, z: 4, core: 2. Of those that a mesh axis runs over, the one named last changes fastest.
Arguments:
- atmosphere: bfloat16 [128, 512, 256], P('lat', 'lon'), may hold values from -6 to 6
- conv_weight: float32 [7, 7, 256], replicated, may hold values from -0.875 to 0.875
- atm_gain: float32 [256], replicated, may hold values from 0.1 to 1.9
- atm_up: bfloat16 [256, 1024], replicated, may hold values from -0.375 to 0.375
- atm_down: bfloat16 [1024, 256], replicated, may hold values from -0.1875 to 0.1875
- flux_weight: bfloat16 [256, 256], replicated, may hold values from -0.375 to 0.375
- land_mask: int32 [128, 512], P('lat', 'lon'), may hold values from 0 to 1, as said below
- tile_owner: int32 [4, 8, 32], P('lat', 'lon'), may hold values from 0 to 31, as said below
- ocean_state: bfloat16 [32, 32, 2, 64, 256], P(('lat', 'lon')), may hold values from -6 to 6
- ocn_gain: float32 [256], replicated, may hold values from 0.1 to 1.9
- ocn_up: bfloat16 [256, 1024], replicated, may hold values from -0.375 to 0.375
- ocn_down: bfloat16 [1024, 256], replicated, may hold values from -0.1875 to 0.1875
Outputs:
- atm_out: bfloat16 [128, 512, 256], P('lat', 'lon')
- ocean_out: bfloat16 [32, 32, 2, 64, 256], P(('lat', 'lon'))
The draws below stay inside these ranges and needn't reach their ends.
Inputs may be any that keep to these rules, and one draw needn't show every extreme that they name: `tile_owner`: each entry is the index along lat+lon (lat slowest) of the device that owns the tile. No device owns more than 2 tiles of one device's block, and one device owns exactly 2 tiles of every device's block. `land_mask`: no bound on the number of ocean cells of a tile or of a device may be relied on.
All inputs are finite; a program needn't handle non-finite values.
Results may differ from the reference program's by a relative error of at most 0.0056.
Values may be sent and summed in bfloat16 or wider, within the bound.
No kernel may reach another device: no remote copies, remote signals or barrier semaphores. Data moves between devices by JAX's collectives and lax.ppermute only.
A program may use at most 64 MiB of HBM per device.

```python
import jax
import jax.numpy as jnp
from jax import lax

C = 256
HID = 1024
KW = 7
CLAT = 32
CLON = 64
CAP = 2
NLAT = 128
NLON = 512
TPD = 32
TILE = 64
N_LON = 8
N_LAT = 4
DEVICES = 32


def draw_land_mask(key, part):
    key_cells, key_tiles, key_forced = jax.random.split(jax.random.fold_in(key, 7), 3)
    cells = (jax.random.randint(key_cells, (NLAT, NLON), 0, 3) < 2).astype(jnp.int32)
    dry_tiles = jax.random.randint(key_tiles, (N_LAT, N_LON, TPD), 0, 16) == 0
    forced = jax.random.randint(key_forced, (N_LAT, N_LON, 1), 0, TPD)
    dry_tiles = dry_tiles | (jnp.arange(TPD, dtype=jnp.int32)[None, None, :] == forced)
    keep_tiles = jnp.where(dry_tiles, 0, 1).astype(jnp.int32)
    keep_cells = jnp.broadcast_to(keep_tiles[:, :, :, None], (N_LAT, N_LON, TPD, TILE))
    keep_cells = keep_cells.reshape(N_LAT, N_LON, CLAT, CLON).transpose(0, 2, 1, 3).reshape(NLAT, NLON)
    return (cells * keep_cells).astype(jnp.int32)


def draw_tile_owner(key, part):
    blocks = N_LAT * N_LON
    slot_count = DEVICES * CAP
    key_favour, key_penalty, key_jitter, key_shuffle = jax.random.split(key, 4)
    favoured = jax.random.randint(key_favour, (), 0, DEVICES)
    penalty = jax.random.randint(key_penalty, (DEVICES,), 0, 4)
    slot_owner = jnp.arange(slot_count, dtype=jnp.int32) // CAP
    jitter = jax.random.randint(key_jitter, (blocks, slot_count), 0, 3072)
    scores = penalty[slot_owner][None, :] * 1024 + jitter
    scores = jnp.where(slot_owner[None, :] == favoured, -1, scores)
    scores = scores * slot_count + jnp.arange(slot_count, dtype=jnp.int32)[None, :]
    ranking = jnp.argsort(scores, axis=1)
    chosen = slot_owner[ranking[:, :TPD]]
    shuffle = jax.random.randint(key_shuffle, (blocks, TPD), 0, 1 << 20) * TPD + jnp.arange(TPD, dtype=jnp.int32)[None, :]
    chosen = jnp.take_along_axis(chosen, jnp.argsort(shuffle, axis=1), axis=1)
    return chosen.reshape(N_LAT, N_LON, TPD).astype(jnp.int32)


def block_levels(stream_key, dims, pieces, low, top_value):
    def one(dim, blocks):
        draws = jax.random.uniform(jax.random.fold_in(jax.random.fold_in(stream_key, 6), dim), (blocks,), jnp.float32, low / len(pieces), top_value / len(pieces))
        return jnp.repeat(jnp.exp(draws), dims[dim] // blocks).reshape((-1,) + (1,) * (len(dims) - dim - 1))

    gain = one(*pieces[0])
    for cut in pieces[1:]:
        gain = gain * one(*cut)
    return gain


def bell_draw(own_key, extent, scale, most, cuts=(), held_as=jnp.bfloat16):
    values = jax.random.normal(own_key, extent, jnp.float32) * scale
    if len(cuts) > 0:
        values = block_levels(own_key, extent, cuts, -0.22, 0.18) * values
    return jnp.clip(values, min=-most, max=most).astype(held_as)


def setup_inputs(seed: int = 0) -> dict:
    streams_of = jax.random.split(jax.random.key(seed), 13)
    atmosphere = bell_draw(streams_of[0], (NLAT, NLON, C), 1.0, 6.0, ((0, 4), (1, 8)))
    conv_weight = bell_draw(streams_of[1], (KW, KW, C), (KW * KW) ** -0.5, 0.875, (), jnp.float32)
    atm_gain = jnp.clip(1.0 + 0.18 * jax.random.normal(streams_of[2], (C,), jnp.float32), 0.1, 1.9)
    atm_up = bell_draw(streams_of[3], (C, HID), C ** -0.5, 0.375)
    atm_down = bell_draw(streams_of[4], (HID, C), HID ** -0.5, 0.1875)
    flux_weight = bell_draw(streams_of[5], (C, C), C ** -0.5, 0.375)
    land_mask = draw_land_mask(jax.random.fold_in(streams_of[12], 71), 0)
    tile_owner = draw_tile_owner(jax.random.fold_in(streams_of[12], 71), 0)
    ocean_state = bell_draw(streams_of[8], (DEVICES, DEVICES, CAP, TILE, C), 1.0, 6.0, ((0, 32),))
    ocn_gain = jnp.clip(1.0 + 0.18 * jax.random.normal(streams_of[9], (C,), jnp.float32), 0.1, 1.9)
    ocn_up = bell_draw(streams_of[10], (C, HID), C ** -0.5, 0.375)
    ocn_down = bell_draw(streams_of[11], (HID, C), HID ** -0.5, 0.1875)
    return dict(atmosphere=atmosphere, conv_weight=conv_weight, atm_gain=atm_gain, atm_up=atm_up, atm_down=atm_down, flux_weight=flux_weight, land_mask=land_mask, tile_owner=tile_owner, ocean_state=ocean_state, ocn_gain=ocn_gain, ocn_up=ocn_up, ocn_down=ocn_down)


def depthwise(padded, kernel, lat_rows, lon_cols):
    summed = jnp.zeros((lat_rows, lon_cols, padded.shape[2]), jnp.float32)
    for row_off in range(kernel.shape[0]):
        for col_off in range(kernel.shape[1]):
            window = padded[row_off:row_off + lat_rows, col_off:col_off + lon_cols, :].astype(jnp.float32)
            summed = summed + window * kernel[row_off, col_off]
    return summed

def normalize(values, scales):
    average = lax.optimization_barrier(jnp.mean(values, axis=-1, keepdims=True))
    centred = values - average
    spread = lax.optimization_barrier(jnp.mean(centred * centred, axis=-1, keepdims=True))
    return centred * lax.rsqrt(spread + 1e-06) * scales

def channel_mixer(values, scales, w_up, w_down):
    normed = normalize(values, scales).astype(jnp.bfloat16)
    hidden = jax.nn.gelu(jnp.dot(normed, w_up, preferred_element_type=jnp.float32), approximate=True).astype(jnp.bfloat16)
    return jnp.dot(hidden, w_down, preferred_element_type=jnp.float32)

def reference(atmosphere, conv_weight, atm_gain, atm_up, atm_down, flux_weight, land_mask, tile_owner, ocean_state, ocn_gain, ocn_up, ocn_down):
    margin = conv_weight.shape[0] // 2
    lon_padded = jnp.pad(atmosphere, ((0, 0), (margin, margin), (0, 0)), mode='wrap')
    padded = jnp.pad(lon_padded, ((margin, margin), (0, 0), (0, 0)))
    mixed = depthwise(padded, conv_weight, NLAT, NLON)

    def atmos_row(carried):
        mixed_row, atmos_in, mask_row = carried
        branch = channel_mixer(mixed_row, atm_gain, atm_up, atm_down)
        out_row = (atmos_in.astype(jnp.float32) + branch).astype(jnp.bfloat16)
        wet_cells = mask_row.astype(jnp.float32)[:, None]
        flux_row = (jnp.dot(out_row, flux_weight, preferred_element_type=jnp.float32) * wet_cells).astype(jnp.bfloat16)
        return (out_row, flux_row)
    atm_out, fluxes = lax.map(atmos_row, (mixed, atmosphere, land_mask))
    flux_tiles = fluxes.reshape(N_LAT, CLAT, N_LON, CLON, C).transpose(0, 2, 1, 3, 4).reshape(DEVICES, TPD, TILE, C)
    owners = tile_owner.reshape(DEVICES, TPD).astype(jnp.int32)
    member = (owners[:, :, None] == jnp.arange(DEVICES, dtype=jnp.int32)[None, None, :]).astype(jnp.int32)
    tile_rank = (lax.optimization_barrier(jnp.sum(jnp.cumsum(member, axis=1) * member, axis=2)) - 1).astype(jnp.int32)
    sources = jnp.broadcast_to(jnp.arange(DEVICES, dtype=jnp.int32)[:, None], owners.shape)
    gathered = ocean_state[owners, sources, tile_rank]

    def ocean_tiles(carried):
        states_in, flux_in = carried
        states = (states_in.astype(jnp.float32) + flux_in.astype(jnp.float32)).reshape(TPD * TILE, C)
        result = states + channel_mixer(states, ocn_gain, ocn_up, ocn_down)
        return result.astype(jnp.bfloat16).reshape(TPD, TILE, C)
    results = lax.map(ocean_tiles, (gathered, flux_tiles))
    ocean_out = jnp.zeros_like(ocean_state).at[owners, sources, tile_rank].set(results)
    return (atm_out, ocean_out)
```

```python
import functools

import jax
import jax.numpy as jnp
from jax import lax
from jax.experimental import pallas as pl
from jax.experimental.pallas import tpu as pltpu
from jax.sharding import PartitionSpec as P

LANES = 128
RIM = 8
VMEM_BYTES = 48 << 20
F32, BF16 = jnp.float32, jnp.bfloat16


def dot(a, b):
    return jnp.dot(a, b, preferred_element_type=F32)


def iota(shape, dim):
    return lax.broadcasted_iota(jnp.int32, shape, dim)


def spread_weights(w_ref, wb, width):
    for h in range(wb.shape[0]):
        for p in range(width):
            for q in range(width):
                row = w_ref[p, q : q + 1, h * LANES : (h + 1) * LANES]
                wb[h, p * width + q] = jnp.broadcast_to(row, (8, LANES))


def conv_kernel(x_ref, w_ref, o_ref, xs, wb):
    rows, cols, _ = x_ref.shape
    width = w_ref.shape[0]
    margin = width // 2
    spread_weights(w_ref, wb, width)
    edge = jnp.zeros((margin,) + xs.shape[1:], F32)
    xs[0:margin] = edge
    xs[rows + margin : rows + 2 * margin] = edge
    side = jnp.zeros((rows, RIM, LANES), F32)
    xs[margin : rows + margin, 0:RIM] = side
    xs[margin : rows + margin, RIM + cols :] = side
    xs[margin : rows + margin, RIM : RIM + cols] = x_ref[...].astype(F32)
    block = 16
    col_blocks = cols // 8

    def body(step, carry):
        r0 = (step // col_blocks) * block
        c0 = pl.multiple_of((step % col_blocks) * 8, 8)
        acc = [None] * block
        for q in range(width):
            shifted = [
                xs[r0 + r, pl.ds(c0 + (RIM - margin + q), 8)] for r in range(block + width - 1)
            ]
            for p in range(width):
                w = wb[0, p * width + q]
                for i in range(block):
                    term = shifted[i + p] * w
                    acc[i] = term if acc[i] is None else acc[i] + term
        for i in range(block):
            o_ref[r0 + i, pl.ds(c0, 8)] = acc[i]
        return carry

    lax.fori_loop(0, (rows // block) * col_blocks, body, 0)


def conv_half(atmosphere, conv_weight, half):
    rows, cols, _ = atmosphere.shape
    width = conv_weight.shape[0]
    margin = width // 2
    return pl.pallas_call(
        conv_kernel,
        out_shape=jax.ShapeDtypeStruct((rows, cols, LANES), F32),
        grid=(1,),
        in_specs=[
            pl.BlockSpec((rows, cols, LANES), lambda i: (0, 0, half)),
            pl.BlockSpec((width, width, LANES), lambda i: (0, 0, half)),
        ],
        out_specs=pl.BlockSpec((rows, cols, LANES), lambda i: (0, 0, 0)),
        scratch_shapes=[
            pltpu.VMEM((rows + 2 * margin, cols + 2 * RIM, LANES), F32),
            pltpu.VMEM((1, width * width, 8, LANES), F32),
        ],
        compiler_params=pltpu.CompilerParams(vmem_limit_bytes=VMEM_BYTES),
        cost_estimate=pl.CostEstimate(
            flops=2 * rows * cols * LANES * width * width, bytes_accessed=6 * rows * cols * LANES, transcendentals=0
        ),
        name="conv_own",
    )(atmosphere, conv_weight)


def widen_kernel(first_ref, last_ref, left_ref, right_ref, up_ref, down_ref):
    margin = up_ref.shape[0]
    rows = left_ref.shape[0]
    cols = first_ref.shape[1]
    skip = last_ref.shape[0] - margin
    for out, body, start, at in (
        (up_ref, first_ref, 0, 0),
        (down_ref, last_ref, skip, rows - margin),
    ):
        out[:, 0:RIM] = left_ref[at : at + margin]
        out[:, RIM : RIM + cols] = body[start : start + margin]
        out[:, RIM + cols :] = right_ref[at : at + margin]


def widen(atmosphere, left, right, margin):
    rows, cols, channels = atmosphere.shape
    blocks = rows // 4
    rim = pl.BlockSpec((rows, RIM, channels), lambda i: (0, 0, 0))
    wide = (margin, cols + 2 * RIM, channels)
    return pl.pallas_call(
        widen_kernel,
        out_shape=[jax.ShapeDtypeStruct(wide, BF16)] * 2,
        grid=(1,),
        in_specs=[
            pl.BlockSpec((4, cols, channels), lambda i: (0, 0, 0)),
            pl.BlockSpec((4, cols, channels), lambda i: (blocks - 1, 0, 0)),
            rim,
            rim,
        ],
        out_specs=[pl.BlockSpec(wide, lambda i: (0, 0, 0))] * 2,
        name="widen_rows",
    )(atmosphere, atmosphere, left, right)


def normalize(values, gain):
    average = jnp.mean(values, axis=-1, keepdims=True)
    centred = values - average
    spread = jnp.mean(centred * centred, axis=-1, keepdims=True)
    return (centred * lax.rsqrt(spread + 1e-06) * gain).astype(BF16)


def mixer(normed, up_ref, down_ref, chunk=256):
    c0 = 0.7978845608028654
    c1 = c0 * 0.044715
    total = None
    for j in range(0, up_ref.shape[1], chunk):
        x = dot(normed, up_ref[:, j : j + chunk])
        gate = jnp.tanh(x * (c0 + c1 * (x * x)))
        hidden = (x + x * gate).astype(BF16)
        part = dot(hidden, down_ref[j : j + chunk, :])
        total = part if total is None else total + part
    return 0.5 * total


def atmosphere_kernel(
    tiles, capacity, tile, owner_sm, mix0_ref, mix1_ref, atm_ref, left_ref, right_ref, top_ref, bottom_ref,
    w_ref, gain_ref, up_ref, down_ref, flux_ref, owner_ref, mask_ref, out_ref, send_ref,
    wb, xl, xr, strip, mixed, fluxes, order_sm, meta,
):
    step, steps = pl.program_id(0), pl.num_programs(0)
    block, cols, channels = atm_ref.shape
    rows = left_ref.shape[0]
    width = w_ref.shape[0]
    margin = width // 2
    halves = channels // LANES
    peers, packed, _ = send_ref.shape
    pair = capacity * tile

    def lanes(h):
        return slice(h * LANES, (h + 1) * LANES)

    @pl.when(step == 0)
    def _():
        spread_weights(w_ref, wb, width)
        for ref in (xl, xr):
            ref[...] = jnp.zeros(ref.shape, F32)
        for h in range(halves):
            xl[h, margin : rows + margin, 0:RIM] = left_ref[:, :, lanes(h)].astype(F32)
            xr[h, margin : rows + margin, RIM:] = right_ref[:, :, lanes(h)].astype(F32)

    for h, mix in enumerate((mix0_ref, mix1_ref)):
        mixed[:, :, lanes(h)] = mix[...]

    for h in range(halves):
        for rim, at, taps in ((xl, 0, range(margin)), (xr, cols - 8, range(margin + 1, width))):
            acc = [None] * block
            for q in taps:
                offset = q + RIM - margin if at == 0 else q - margin
                shifted = [rim[h, step * block + r, offset : offset + 8] for r in range(block + width - 1)]
                for p in range(width):
                    w = wb[h, p * width + q]
                    for i in range(block):
                        term = shifted[i + p] * w
                        acc[i] = term if acc[i] is None else acc[i] + term
            for i in range(block):
                mixed[i, at : at + 8, lanes(h)] += acc[i]

    def latitude(rows_ref, pairs):
        for h in range(halves):
            strip[h] = rows_ref[:, :, lanes(h)].astype(F32)

        def body(c, carry):
            c0 = pl.multiple_of(c * 8, 8)
            for h in range(halves):
                for i, taps in pairs:
                    acc = mixed[i, pl.ds(c0, 8), lanes(h)]
                    for row, p in taps:
                        for q in range(width):
                            acc += strip[h, row, pl.ds(c0 + (RIM - margin + q), 8)] * wb[h, p * width + q]
                    mixed[i, pl.ds(c0, 8), lanes(h)] = acc
            return carry

        lax.fori_loop(0, cols // 8, body, 0)

    @pl.when(step == 0)
    def _():
        latitude(top_ref, [(i, [(i + p, p) for p in range(margin - i)]) for i in range(margin)])

    @pl.when(step == steps - 1)
    def _():
        latitude(
            bottom_ref,
            [
                (block - margin + i, [(i - e, width - 1 - e) for e in range(i + 1)])
                for i in range(margin)
            ],
        )

    cells = block * cols
    normed = normalize(mixed[...].reshape(cells, channels), gain_ref[...])
    branch = mixer(normed, up_ref, down_ref)
    new = (atm_ref[...].reshape(cells, channels).astype(F32) + branch).astype(BF16)
    out_ref[...] = new.reshape(block, cols, channels)
    fluxes[pl.ds(pl.multiple_of(step * cells, cells), cells), :] = dot(new, flux_ref[...]).astype(BF16)

    @pl.when(step == steps - 1)
    def _():
        member = (owner_ref[...] == iota((peers, tiles), 0)).astype(F32)
        before = (iota((tiles, tiles), 0) < iota((tiles, tiles), 1)).astype(BF16)
        rank = dot(member.astype(BF16), before)
        bits = jnp.zeros((peers, LANES), F32)
        flags = jnp.zeros((peers, LANES), F32)
        lane = iota((peers, LANES), 1)
        for r in range(capacity):
            chosen = jnp.where(rank == float(r), member, 0.0)
            bits += dot(chosen.astype(BF16), mask_ref[:, r * LANES : (r + 1) * LANES])
            flags += jnp.where(lane == r, jnp.sum(chosen, axis=1, keepdims=True), 0.0)
        over = jnp.max(jnp.sum(bits, axis=1, keepdims=True), axis=0, keepdims=True) > float(packed - 1)
        flags += jnp.where((lane == capacity) & over, 1.0, 0.0)
        meta[:, 0:LANES] = bits
        meta[:, LANES:] = flags
        ahead = jnp.where(
            iota((LANES, LANES), 0) < iota((LANES, LANES), 1),
            1.0,
            jnp.where(iota((LANES, LANES), 0) == iota((LANES, LANES), 1), 1000.0, 0.0),
        ).astype(BF16)
        place = (dot(bits.astype(BF16), ahead) - 999.0).astype(jnp.int32)

        def clear(o, carry):
            for r in range(capacity):
                order_sm[o * capacity + r] = 0
            order_sm[peers * capacity + o] = 0
            return carry

        lax.fori_loop(0, peers, clear, 0)

        def count(t, carry):
            o = owner_sm[t]
            r = order_sm[peers * capacity + o]
            order_sm[o * capacity + r] = t
            order_sm[peers * capacity + o] = r + 1
            return carry

        lax.fori_loop(0, tiles, count, 0)
        order = iota((packed, LANES), 0)
        for o in range(peers):
            held = [
                fluxes[pl.ds(pl.multiple_of(order_sm[o * capacity + r] * tile, tile), tile), :]
                for r in range(capacity)
            ]
            pick = jnp.where(order == place[o : o + 1, :], 1.0, 0.0).astype(BF16)
            packet = dot(pick[:, 0:pair], jnp.concatenate(held, axis=0))
            head = iota((packed, channels), 0) == 0
            send_ref[o] = jnp.where(head, meta[o : o + 1, :], packet).astype(BF16)


def atmosphere_step(
    mix0, mix1, atmosphere, left, right, top, bottom, conv_weight, gain, w_up, w_down, w_flux, owners, mask, peers,
    capacity, tile, packed,
):
    rows, cols, channels = atmosphere.shape
    tiles = owners.shape[0]
    width = conv_weight.shape[0]
    margin = width // 2
    block = 8
    halves = channels // LANES
    hidden = w_up.shape[1]
    tile_bits = mask.reshape(tiles, tile).astype(BF16)
    bits = jnp.concatenate(
        [jnp.pad(tile_bits, ((0, 0), (r * tile, LANES - (r + 1) * tile))) for r in range(capacity)], axis=1
    )

    def whole(shape):
        return pl.BlockSpec(shape, lambda i, *_: (0,) * len(shape))

    def by_rows(last):
        return pl.BlockSpec((block, cols, last), lambda i, *_: (i, 0, 0))

    cells = rows * cols
    return pl.pallas_call(
        functools.partial(atmosphere_kernel, tiles, capacity, tile),
        out_shape=[
            jax.ShapeDtypeStruct((rows, cols, channels), BF16),
            jax.ShapeDtypeStruct((peers, packed, channels), BF16),
        ],
        grid_spec=pltpu.PrefetchScalarGridSpec(
            num_scalar_prefetch=1,
            grid=(rows // block,),
            in_specs=[
                by_rows(LANES),
                by_rows(LANES),
                by_rows(channels),
                whole((rows, RIM, channels)),
                whole((rows, RIM, channels)),
                whole((margin, cols + 2 * RIM, channels)),
                whole((margin, cols + 2 * RIM, channels)),
                whole((width, width, channels)),
                whole((1, channels)),
                whole((channels, hidden)),
                whole((hidden, channels)),
                whole((channels, channels)),
                whole((1, tiles)),
                whole((tiles, capacity * LANES)),
            ],
            out_specs=[by_rows(channels), whole((peers, packed, channels))],
            scratch_shapes=[
                pltpu.VMEM((halves, width * width, 8, LANES), F32),
                pltpu.VMEM((halves, rows + 2 * margin, 2 * RIM, LANES), F32),
                pltpu.VMEM((halves, rows + 2 * margin, 2 * RIM, LANES), F32),
                pltpu.VMEM((halves, margin, cols + 2 * RIM, LANES), F32),
                pltpu.VMEM((block, cols, channels), F32),
                pltpu.VMEM((cells, channels), BF16),
                pltpu.SMEM((peers * (capacity + 1),), jnp.int32),
                pltpu.VMEM((peers, 2 * LANES), F32),
            ],
        ),
        compiler_params=pltpu.CompilerParams(vmem_limit_bytes=VMEM_BYTES),
        cost_estimate=pl.CostEstimate(
            flops=2 * cells * channels * (2 * hidden + channels), bytes_accessed=12 * cells * channels,
            transcendentals=cells * hidden,
        ),
        name="atmosphere",
    )(
        owners, mix0, mix1, atmosphere, left, right, top, bottom, conv_weight, gain.reshape(1, -1), w_up, w_down,
        w_flux, owners.reshape(1, -1), bits,
    )


def ocean_kernel(capacity, state_ref, packet_ref, gain_ref, up_ref, down_ref, out_ref):
    group, pair, channels = state_ref.shape
    packed = packet_ref.shape[1]
    tile = pair // capacity
    head = jnp.concatenate([packet_ref[g, 0:1, :] for g in range(group)], axis=0)
    ahead = jnp.where(
        iota((pair, LANES), 1) < iota((pair, LANES), 0),
        1.0,
        jnp.where(iota((pair, LANES), 1) == iota((pair, LANES), 0), 1000.0, 0.0),
    ).astype(BF16)
    place = lax.dot_general(
        ahead, head[:, 0:LANES], (((1,), (1,)), ((), ())), preferred_element_type=F32
    )
    place = (place - 999.0).astype(jnp.int32)
    order = iota((pair, packed), 1)
    states = []
    for g in range(group):
        pick = jnp.where(order == place[:, g : g + 1], 1.0, 0.0).astype(BF16)
        states.append(state_ref[g].astype(F32) + dot(pick, packet_ref[g]))
    states = jnp.concatenate(states, axis=0)
    result = states + mixer(normalize(states, gain_ref[...]), up_ref, down_ref)
    for g in range(group):
        for r in range(capacity):
            used = head[g : g + 1, LANES + r : LANES + r + 1].astype(F32) > 0.0
            at = g * pair + r * tile
            part = jnp.where(used, result[at : at + tile], 0.0)
            out_ref[g, r * tile : (r + 1) * tile, :] = part.astype(BF16)


def ocean_step(state, packets, gain, w_up, w_down, capacity):
    peers, pair, channels = state.shape
    packed = packets.shape[1]
    hidden = w_up.shape[1]
    group = 512 // pair

    def whole(shape):
        return pl.BlockSpec(shape, lambda i: (0,) * len(shape))

    cells = peers * pair
    return pl.pallas_call(
        functools.partial(ocean_kernel, capacity),
        out_shape=jax.ShapeDtypeStruct((peers, pair, channels), BF16),
        grid=(peers // group,),
        in_specs=[
            pl.BlockSpec((group, pair, channels), lambda i: (i, 0, 0)),
            pl.BlockSpec((group, packed, channels), lambda i: (i, 0, 0)),
            whole((1, channels)),
            whole((channels, hidden)),
            whole((hidden, channels)),
        ],
        out_specs=pl.BlockSpec((group, pair, channels), lambda i: (i, 0, 0)),
        compiler_params=pltpu.CompilerParams(vmem_limit_bytes=VMEM_BYTES),
        cost_estimate=pl.CostEstimate(
            flops=4 * cells * channels * hidden, bytes_accessed=6 * cells * channels, transcendentals=cells * hidden
        ),
        name="ocean",
    )(state, packets, gain.reshape(1, -1), w_up, w_down)


def full_exchange(atm_out, w_flux, mask, owners, state, gain, w_up, w_down, capacity):
    rows, cols, channels = atm_out.shape
    peers, pair, _ = state.shape
    tile = pair // capacity
    wet = mask.reshape(-1, 1).astype(F32)
    fluxes = (dot(atm_out.reshape(-1, channels), w_flux) * wet).astype(BF16)
    member = (owners[:, None] == jnp.arange(peers, dtype=jnp.int32)[None, :]).astype(jnp.int32)
    rank = jnp.sum(jnp.cumsum(member, axis=0) * member, axis=1) - 1
    slot = owners * capacity + rank
    slots = peers * capacity
    out = jnp.zeros((slots, tile, channels), BF16).at[slot].set(fluxes.reshape(-1, tile, channels))
    used = jnp.zeros((slots,), BF16).at[slot].set(1.0)
    out = out.reshape(peers, pair, channels)
    used = used.reshape(peers, capacity)
    arrived = lax.all_to_all(out, ("lat", "lon"), split_axis=0, concat_axis=0, tiled=True)
    filled = lax.all_to_all(used, ("lat", "lon"), split_axis=0, concat_axis=0, tiled=True)
    values = (state.astype(F32) + arrived.astype(F32)).reshape(peers * pair, channels)
    normed = normalize(values, gain)
    hidden = jax.nn.gelu(dot(normed, w_up), approximate=True).astype(BF16)
    result = (values + dot(hidden, w_down)).reshape(peers, capacity, tile, channels)
    result = result * filled.astype(F32)[:, :, None, None]
    return result.astype(BF16).reshape(peers, pair, channels)


def per_device(
    atmosphere,
    conv_weight,
    atm_gain,
    atm_up,
    atm_down,
    flux_weight,
    land_mask,
    tile_owner,
    ocean_state,
    ocn_gain,
    ocn_up,
    ocn_down,
):
    margin = conv_weight.shape[0] // 2
    channels = atmosphere.shape[2]
    _, peers, capacity, tile, _ = ocean_state.shape
    pair = capacity * tile
    packed = -(-(pair * 13 // 16) // 8) * 8
    n_lon, n_lat = lax.axis_size("lon"), lax.axis_size("lat")
    owners = tile_owner.reshape(-1)
    state = ocean_state.reshape(peers, pair, channels)

    around = [(i, (i + 1) % n_lon) for i in range(n_lon)]
    left = lax.ppermute(atmosphere[:, -RIM:], "lon", around)
    right = lax.ppermute(atmosphere[:, :RIM], "lon", [(j, i) for i, j in around])
    mix0 = conv_half(atmosphere, conv_weight, 0)
    mix1 = conv_half(atmosphere, conv_weight, 1)
    up, down = widen(atmosphere, left, right, margin)
    north = [(i, i + 1) for i in range(n_lat - 1)]
    top = lax.ppermute(down, "lat", north)
    bottom = lax.ppermute(up, "lat", [(j, i) for i, j in north])

    atm_out, packets = atmosphere_step(
        mix0, mix1, atmosphere, left, right, top, bottom, conv_weight, atm_gain, atm_up, atm_down, flux_weight,
        owners, land_mask, peers, capacity, tile, packed,
    )
    arrived = lax.all_to_all(packets, ("lat", "lon"), split_axis=0, concat_axis=0, tiled=True)
    over = jnp.max(arrived[:, 0, LANES + capacity]) > 0
    ocean_out = lax.cond(
        over,
        lambda: full_exchange(
            atm_out, flux_weight, land_mask, owners, state, ocn_gain, ocn_up, ocn_down, capacity
        ),
        lambda: ocean_step(state, arrived, ocn_gain, ocn_up, ocn_down, capacity),
    )
    return atm_out, ocean_out.reshape(ocean_state.shape)


def solution(mesh):
    placed = (
        P("lat", "lon", None),
        P(),
        P(),
        P(),
        P(),
        P(),
        P("lat", "lon"),
        P("lat", "lon", None),
        P(("lat", "lon"), None, None, None, None),
        P(),
        P(),
        P(),
    )
    return jax.shard_map(
        per_device,
        mesh=mesh,
        in_specs=placed,
        out_specs=(P("lat", "lon", None), P(("lat", "lon"), None, None, None, None)),
        check_vma=False,
    )
```

```python
import functools

import jax
import jax.numpy as jnp
from jax import lax
from jax.experimental import pallas as pl
from jax.experimental.pallas import tpu as pltpu
from jax.sharding import PartitionSpec as P

LANES = 128
RIM = 8
VMEM_BYTES = 48 << 20
F32, BF16 = jnp.float32, jnp.bfloat16
ANY = pl.BlockSpec(memory_space=pl.ANY)
IN_VMEM = pl.BlockSpec(memory_space=pltpu.VMEM)


def hbm(x):
    return pltpu.with_memory_space_constraint(x, pltpu.HBM)


def vmem(x):
    return pltpu.with_memory_space_constraint(x, pltpu.VMEM)


def dot(a, b):
    return jnp.dot(a, b, preferred_element_type=F32)


def iota(shape, dim):
    return lax.broadcasted_iota(jnp.int32, shape, dim)


def spread_weights(w_ref, wb, width):
    for h in range(wb.shape[0]):
        for p in range(width):
            for q in range(width):
                row = w_ref[p, q : q + 1, h * LANES : (h + 1) * LANES]
                wb[h, p * width + q] = jnp.broadcast_to(row, (8, LANES))


def taps_sum(read, wb, h, rows, width):
    total = [None] * rows
    for q in range(width):
        window = [read(r, q) for r in range(rows + width - 1)]
        for p in range(width):
            w = wb[h, p * width + q]
            for i in range(rows):
                term = window[i + p] * w
                total[i] = term if total[i] is None else total[i] + term
    return total


def inner_kernel(x_ref, w_ref, mixed_ref, own_ref, xs, wb, sem):
    rows, cols, channels = own_ref.shape
    width = w_ref.shape[0]
    margin = width // 2
    fetch = pltpu.make_async_copy(x_ref, own_ref, sem)
    fetch.start()
    spread_weights(w_ref, wb, width)
    halves = channels // LANES
    zero = jnp.zeros((halves, margin) + xs.shape[2:], F32)
    xs[:, 0:margin] = zero
    xs[:, rows + margin :] = zero
    fetch.wait()
    for h in range(halves):
        xs[h, margin : rows + margin] = own_ref[:, :, h * LANES : (h + 1) * LANES].astype(F32)
    block = 16
    blocks = (cols - 2 * RIM) // 8

    def body(step, carry):
        r0 = (step // blocks) * block
        c0 = pl.multiple_of((step % blocks) * 8, 8)
        for h in range(halves):
            total = taps_sum(
                lambda r, q: xs[h, r0 + r, pl.ds(c0 + (RIM - margin + q), 8)], wb, h, block, width
            )
            for i in range(block):
                mixed_ref[h, r0 + i, pl.ds(c0 + RIM, 8)] = total[i]
        return carry

    lax.fori_loop(0, (rows // block) * blocks, body, 0)


def conv_inner(atmosphere, conv_weight):
    rows, cols, channels = atmosphere.shape
    width = conv_weight.shape[0]
    margin = width // 2
    halves = channels // LANES
    return pl.pallas_call(
        inner_kernel,
        out_shape=[
            pltpu.VMEM((halves, rows, cols, LANES), F32),
            pltpu.VMEM((rows, cols, channels), BF16),
        ],
        in_specs=[ANY, IN_VMEM],
        out_specs=[IN_VMEM, IN_VMEM],
        scratch_shapes=[
            pltpu.VMEM((halves, rows + 2 * margin, cols, LANES), F32),
            pltpu.VMEM((halves, width * width, 8, LANES), F32),
            pltpu.SemaphoreType.DMA,
        ],
        compiler_params=pltpu.CompilerParams(vmem_limit_bytes=VMEM_BYTES),
        cost_estimate=pl.CostEstimate(
            flops=2 * rows * cols * channels * width * width, bytes_accessed=6 * rows * cols * channels, transcendentals=0
        ),
        name="conv_inner",
    )(hbm(atmosphere), hbm(conv_weight))


def outer_kernel(
    mixed_in, own_ref, left_ref, right_ref, w_ref, *refs, count
):
    far, mixed_ref, near = refs[:count], refs[count], refs[count + 1 : 2 * count + 1]
    xs, wb, sems = refs[2 * count + 1 :]
    fetches = [pltpu.make_async_copy(f, n, sems.at[i]) for i, (f, n) in enumerate(zip(far, near))]
    for fetch in fetches:
        fetch.start()
    rows, cols, channels = own_ref.shape
    width = w_ref.shape[0]
    margin = width // 2
    halves = channels // LANES
    spread_weights(w_ref, wb, width)
    zero = jnp.zeros((2, margin) + xs.shape[2:], F32)
    xs[:, 0:margin] = zero
    xs[:, rows + margin :] = zero
    own = slice(margin, rows + margin)
    block = 16
    for h in range(halves):
        part = slice(h * LANES, (h + 1) * LANES)
        xs[0, own, 0:RIM] = left_ref[:, :, part].astype(F32)
        xs[0, own, RIM:] = own_ref[:, 0 : 2 * RIM, part].astype(F32)
        xs[1, own, 0 : 2 * RIM] = own_ref[:, cols - 2 * RIM :, part].astype(F32)
        xs[1, own, 2 * RIM :] = right_ref[:, :, part].astype(F32)

        def body(step, carry):
            r0 = step * block
            for side in range(2):
                total = taps_sum(
                    lambda r, q: xs[side, r0 + r, RIM - margin + q : 2 * RIM - margin + q], wb, h, block, width
                )
                at = side * (cols - RIM)
                for i in range(block):
                    mixed_ref[h, r0 + i, at : at + RIM] = total[i]
            return carry

        lax.fori_loop(0, rows // block, body, 0)
    for fetch in fetches:
        fetch.wait()


def conv_outer(mixed, own, left, right, conv_weight, weights):
    rows, cols, channels = own.shape
    width = conv_weight.shape[0]
    margin = width // 2
    halves = channels // LANES
    count = len(weights)
    return pl.pallas_call(
        functools.partial(outer_kernel, count=count),
        out_shape=[pltpu.VMEM(mixed.shape, F32)] + [pltpu.VMEM(w.shape, w.dtype) for w in weights],
        in_specs=[IN_VMEM] * 5 + [ANY] * count,
        out_specs=[IN_VMEM] * (count + 1),
        input_output_aliases={0: 0},
        scratch_shapes=[
            pltpu.VMEM((2, rows + 2 * margin, 3 * RIM, LANES), F32),
            pltpu.VMEM((halves, width * width, 8, LANES), F32),
            pltpu.SemaphoreType.DMA((count,)),
        ],
        compiler_params=pltpu.CompilerParams(vmem_limit_bytes=VMEM_BYTES),
        cost_estimate=pl.CostEstimate(
            flops=4 * rows * RIM * channels * width * width, bytes_accessed=12 * rows * RIM * channels, transcendentals=0
        ),
        name="conv_outer",
    )(vmem(mixed), vmem(own), vmem(left), vmem(right), hbm(conv_weight), *[hbm(w) for w in weights])


def widen_kernel(own_ref, left_ref, right_ref, up_ref, down_ref):
    margin = up_ref.shape[0]
    rows, cols, _ = own_ref.shape
    for out, at in ((up_ref, 0), (down_ref, rows - margin)):
        out[:, 0:RIM] = left_ref[at : at + margin]
        out[:, RIM : RIM + cols] = own_ref[at : at + margin]
        out[:, RIM + cols :] = right_ref[at : at + margin]


def widen(own, left, right, margin):
    rows, cols, channels = own.shape
    return pl.pallas_call(
        widen_kernel,
        out_shape=[pltpu.VMEM((margin, cols + 2 * RIM, channels), BF16)] * 2,
        in_specs=[IN_VMEM] * 3,
        out_specs=[IN_VMEM] * 2,
        compiler_params=pltpu.CompilerParams(vmem_limit_bytes=VMEM_BYTES),
        name="widen_rows",
    )(vmem(own), vmem(left), vmem(right))


def normalize(values, gain):
    average = jnp.mean(values, axis=-1, keepdims=True)
    centred = values - average
    spread = jnp.mean(centred * centred, axis=-1, keepdims=True)
    return (centred * lax.rsqrt(spread + 1e-06) * gain).astype(BF16)


def mixer(normed, up_ref, down_ref, chunk=256):
    c0 = 0.7978845608028654
    c1 = c0 * 0.044715
    total = None
    for j in range(0, up_ref.shape[1], chunk):
        x = dot(normed, up_ref[:, j : j + chunk])
        gate = jnp.tanh(x * (c0 + c1 * (x * x)))
        hidden = (x + x * gate).astype(BF16)
        part = dot(hidden, down_ref[j : j + chunk, :])
        total = part if total is None else total + part
    return 0.5 * total


def atmosphere_kernel(
    tiles, capacity, tile, owner_sm, mixed_in, atm_ref, top_ref, bottom_ref, w_ref, gain_ref, up_ref, down_ref,
    flux_ref, owner_ref, mask_ref, out_ref, send_ref, mark_ref, mixed_ref,
    wb, strip, fluxes, order_sm, meta, places, new_out, packets, out_sems, send_sems,
):
    rows, cols, channels = atm_ref.shape
    width = w_ref.shape[0]
    margin = width // 2
    halves = channels // LANES
    peers, packed, _ = send_ref.shape
    pair = capacity * tile

    def lanes(h):
        return slice(h * LANES, (h + 1) * LANES)

    spread_weights(w_ref, wb, width)

    def latitude(rows_ref, pairs):
        for h in range(halves):
            strip[h] = rows_ref[:, :, lanes(h)].astype(F32)

        def body(c, carry):
            c0 = pl.multiple_of(c * 8, 8)
            for h in range(halves):
                for i, taps in pairs:
                    acc = mixed_ref[h, i, pl.ds(c0, 8)]
                    for row, p in taps:
                        for q in range(width):
                            acc += strip[h, row, pl.ds(c0 + (RIM - margin + q), 8)] * wb[h, p * width + q]
                    mixed_ref[h, i, pl.ds(c0, 8)] = acc
            return carry

        lax.fori_loop(0, cols // 8, body, 0)

    latitude(top_ref, [(i, [(i + p, p) for p in range(margin - i)]) for i in range(margin)])
    latitude(
        bottom_ref,
        [
            (rows - margin + i, [(i - e, width - 1 - e) for e in range(i + 1)])
            for i in range(margin)
        ],
    )

    block = 16
    cells = block * cols

    def leave(step):
        part = pl.ds(step * block, block)
        return pltpu.make_async_copy(new_out.at[part], out_ref.at[part], out_sems.at[step])

    def mix(step, carry):
        r0 = step * block
        parts = [mixed_ref[h, pl.ds(r0, block)].reshape(cells, LANES) for h in range(halves)]
        normed = normalize(jnp.concatenate(parts, axis=1), gain_ref[...])
        branch = mixer(normed, up_ref, down_ref)
        new = (atm_ref[pl.ds(r0, block)].reshape(cells, channels).astype(F32) + branch).astype(BF16)
        new_out[pl.ds(r0, block)] = new.reshape(block, cols, channels)
        leave(step).start()
        fluxes[pl.ds(pl.multiple_of(step * cells, cells), cells), :] = dot(new, flux_ref[...]).astype(BF16)
        return carry

    lax.fori_loop(0, rows // block, mix, 0)

    member = (owner_ref[...] == iota((peers, tiles), 0)).astype(F32)
    before = (iota((tiles, tiles), 0) < iota((tiles, tiles), 1)).astype(BF16)
    rank = dot(member.astype(BF16), before)
    bits = jnp.zeros((peers, LANES), F32)
    flags = jnp.zeros((peers, LANES), F32)
    lane = iota((peers, LANES), 1)
    for r in range(capacity):
        chosen = jnp.where(rank == float(r), member, 0.0)
        at = (iota((tile, LANES), 1) == iota((tile, LANES), 0) + r * tile).astype(BF16)
        shifted = dot(mask_ref[...].astype(F32).astype(BF16), at).astype(BF16)
        bits += dot(chosen.astype(BF16), shifted)
        flags += jnp.where(lane == r, jnp.sum(chosen, axis=1, keepdims=True), 0.0)
    over = jnp.max(jnp.sum(bits, axis=1, keepdims=True), axis=0, keepdims=True) > float(packed - 1)
    flags += jnp.where((lane == capacity) & over, 1.0, 0.0)
    meta[:, 0:LANES] = bits
    meta[:, LANES:] = flags
    ahead = jnp.where(
        iota((LANES, LANES), 0) < iota((LANES, LANES), 1),
        1.0,
        jnp.where(iota((LANES, LANES), 0) == iota((LANES, LANES), 1), 1000.0, 0.0),
    ).astype(BF16)
    places[...] = (dot(bits.astype(BF16), ahead) - 999.0).astype(jnp.int32)

    def clear(o, carry):
        for r in range(capacity):
            order_sm[o * capacity + r] = 0
        order_sm[peers * capacity + o] = 0
        return carry

    lax.fori_loop(0, peers, clear, 0)

    def count(t, carry):
        o = owner_sm[t]
        r = order_sm[peers * capacity + o]
        order_sm[o * capacity + r] = t
        order_sm[peers * capacity + o] = r + 1
        return carry

    lax.fori_loop(0, tiles, count, 0)
    order = iota((packed, LANES), 0)
    top_row = iota((packed, channels), 0) == 0
    group = peers // 4

    def send(i):
        part = pl.ds(i * group, group)
        return pltpu.make_async_copy(packets.at[part], send_ref.at[part], send_sems.at[i])

    def pack(i, carry):
        for k in range(group):
            o = i * group + k
            held = [
                fluxes[pl.ds(pl.multiple_of(order_sm[o * capacity + r] * tile, tile), tile), :]
                for r in range(capacity)
            ]
            pick = jnp.where(order == places[pl.ds(o, 1), :], 1.0, 0.0).astype(BF16)
            packet = dot(pick[:, 0:pair], jnp.concatenate(held, axis=0))
            packets[o] = jnp.where(top_row, meta[pl.ds(o, 1), :], packet).astype(BF16)
        send(i).start()
        return carry

    lax.fori_loop(0, 4, pack, 0)
    mark_ref[...] = jnp.zeros(mark_ref.shape, F32)
    for step in range(rows // block):
        leave(step).wait()
    for i in range(4):
        send(i).wait()


def atmosphere_step(
    mixed, own, top, bottom, conv_weight, gain, w_up, w_down, w_flux, owners, mask, peers, capacity, tile, packed
):
    rows, cols, channels = own.shape
    tiles = owners.shape[0]
    width = conv_weight.shape[0]
    margin = width // 2
    halves = channels // LANES
    hidden = w_up.shape[1]
    cells = rows * cols
    in_smem = pl.BlockSpec(memory_space=pltpu.SMEM)
    return pl.pallas_call(
        functools.partial(atmosphere_kernel, tiles, capacity, tile),
        out_shape=[
            jax.ShapeDtypeStruct((rows, cols, channels), BF16),
            jax.ShapeDtypeStruct((peers, packed, channels), BF16),
            jax.ShapeDtypeStruct((8, LANES), F32),
            pltpu.VMEM(mixed.shape, F32),
        ],
        in_specs=[in_smem] + [IN_VMEM] * 11,
        out_specs=[ANY, ANY, IN_VMEM, IN_VMEM],
        input_output_aliases={1: 3},
        scratch_shapes=[
            pltpu.VMEM((halves, width * width, 8, LANES), F32),
            pltpu.VMEM((halves, margin, cols + 2 * RIM, LANES), F32),
            pltpu.VMEM((cells, channels), BF16),
            pltpu.SMEM((peers * (capacity + 1),), jnp.int32),
            pltpu.VMEM((peers, 2 * LANES), F32),
            pltpu.VMEM((peers, LANES), jnp.int32),
            pltpu.VMEM((rows, cols, channels), BF16),
            pltpu.VMEM((peers, packed, channels), BF16),
            pltpu.SemaphoreType.DMA((rows,)),
            pltpu.SemaphoreType.DMA((4,)),
        ],
        compiler_params=pltpu.CompilerParams(vmem_limit_bytes=VMEM_BYTES),
        cost_estimate=pl.CostEstimate(
            flops=2 * cells * channels * (2 * hidden + channels), bytes_accessed=12 * cells * channels,
            transcendentals=cells * hidden,
        ),
        name="atmosphere",
    )(
        owners, vmem(mixed), vmem(own), vmem(top), vmem(bottom), hbm(conv_weight), gain.reshape(1, -1), vmem(w_up),
        vmem(w_down), vmem(w_flux), owners.reshape(1, -1), mask,
    )


def fetch_kernel(mark_ref, *refs):
    count = (len(refs) - 1) // 2
    copies = [
        pltpu.make_async_copy(refs[i], refs[count + i], refs[-1].at[i]) for i in range(count)
    ]
    for copy in copies:
        copy.start()
    for copy in copies:
        copy.wait()


def fetch(mark, arrays):
    return pl.pallas_call(
        fetch_kernel,
        out_shape=[pltpu.VMEM(x.shape, x.dtype) for x in arrays],
        in_specs=[ANY] * (len(arrays) + 1),
        out_specs=[IN_VMEM] * len(arrays),
        scratch_shapes=[pltpu.SemaphoreType.DMA((len(arrays),))],
        compiler_params=pltpu.CompilerParams(vmem_limit_bytes=VMEM_BYTES),
        name="fetch",
    )(mark, *[hbm(x) for x in arrays])


def ocean_kernel(
    capacity, chain, state_ref, packet_hbm, gain_ref, up_ref, down_ref, out_hbm, over_ref, packet_ref, out_ref,
    in_sems, out_sems,
):
    peers, pair, channels = state_ref.shape
    packed = packet_ref.shape[1]
    tile = pair // capacity
    chains = peers // chain

    def arrive(i):
        part = pl.ds(i * chain, chain)
        return pltpu.make_async_copy(packet_hbm.at[part], packet_ref.at[part], in_sems.at[i])

    def leave(i):
        part = pl.ds(i * chain, chain)
        return pltpu.make_async_copy(out_ref.at[part], out_hbm.at[part], out_sems.at[i])

    for i in range(chains):
        arrive(i).start()
    ahead = jnp.where(
        iota((pair, LANES), 1) < iota((pair, LANES), 0),
        1.0,
        jnp.where(iota((pair, LANES), 1) == iota((pair, LANES), 0), 1000.0, 0.0),
    ).astype(BF16)
    order = iota((pair, packed), 1)

    def mix(i, over):
        arrive(i).wait()
        first = i * chain
        head = jnp.concatenate([packet_ref[first + g, 0:1, :] for g in range(chain)], axis=0)
        place = lax.dot_general(
            ahead, head[:, 0:LANES], (((1,), (1,)), ((), ())), preferred_element_type=F32
        )
        place = (place - 999.0).astype(jnp.int32)
        flags = head[:, LANES:].astype(F32)
        states = []
        for g in range(chain):
            pick = jnp.where(order == place[:, g : g + 1], 1.0, 0.0).astype(BF16)
            states.append(state_ref[first + g].astype(F32) + dot(pick, packet_ref[first + g]))
        states = jnp.concatenate(states, axis=0)
        result = states + mixer(normalize(states, gain_ref[...]), up_ref, down_ref)
        for g in range(chain):
            for r in range(capacity):
                used = flags[g : g + 1, r : r + 1] > 0.0
                at = g * pair + r * tile
                part = jnp.where(used, result[at : at + tile], 0.0)
                out_ref[first + g, r * tile : (r + 1) * tile, :] = part.astype(BF16)
        leave(i).start()
        return jnp.maximum(over, jnp.max(flags[:, capacity : capacity + 1], axis=0, keepdims=True))

    over = lax.fori_loop(0, chains, mix, jnp.zeros((1, 1), F32))
    over_ref[0, 0] = jnp.max(over)
    for i in range(chains):
        leave(i).wait()


def ocean_step(state, packets, gain, w_up, w_down, capacity):
    peers, pair, channels = state.shape
    packed = packets.shape[1]
    hidden = w_up.shape[1]
    chain = min(peers, 1024 // pair)
    chains = peers // chain
    cells = peers * pair
    return pl.pallas_call(
        functools.partial(ocean_kernel, capacity, chain),
        out_shape=[
            jax.ShapeDtypeStruct((peers, pair, channels), BF16),
            jax.ShapeDtypeStruct((1, 1), F32),
        ],
        in_specs=[IN_VMEM, ANY, IN_VMEM, IN_VMEM, IN_VMEM],
        out_specs=[ANY, pl.BlockSpec(memory_space=pltpu.SMEM)],
        scratch_shapes=[
            pltpu.VMEM((peers, packed, channels), BF16),
            pltpu.VMEM((peers, pair, channels), BF16),
            pltpu.SemaphoreType.DMA((chains,)),
            pltpu.SemaphoreType.DMA((chains,)),
        ],
        compiler_params=pltpu.CompilerParams(vmem_limit_bytes=VMEM_BYTES),
        cost_estimate=pl.CostEstimate(
            flops=4 * cells * channels * hidden, bytes_accessed=6 * cells * channels, transcendentals=cells * hidden
        ),
        name="ocean",
    )(vmem(state), hbm(packets), gain, vmem(w_up), vmem(w_down))


def full_exchange(atm_out, w_flux, mask, owners, state, gain, w_up, w_down, capacity):
    rows, cols, channels = atm_out.shape
    peers, pair, _ = state.shape
    tile = pair // capacity
    wet = mask.reshape(-1, 1).astype(F32)
    fluxes = (dot(atm_out.reshape(-1, channels), w_flux) * wet).astype(BF16)
    member = (owners[:, None] == jnp.arange(peers, dtype=jnp.int32)[None, :]).astype(jnp.int32)
    rank = jnp.sum(jnp.cumsum(member, axis=0) * member, axis=1) - 1
    slot = owners * capacity + rank
    slots = peers * capacity
    out = jnp.zeros((slots, tile, channels), BF16).at[slot].set(fluxes.reshape(-1, tile, channels))
    used = jnp.zeros((slots,), BF16).at[slot].set(1.0)
    out = out.reshape(peers, pair, channels)
    used = used.reshape(peers, capacity)
    arrived = lax.all_to_all(out, ("lat", "lon"), split_axis=0, concat_axis=0, tiled=True)
    filled = lax.all_to_all(used, ("lat", "lon"), split_axis=0, concat_axis=0, tiled=True)
    values = (state.astype(F32) + arrived.astype(F32)).reshape(peers * pair, channels)
    normed = normalize(values, gain)
    hidden = jax.nn.gelu(dot(normed, w_up), approximate=True).astype(BF16)
    result = (values + dot(hidden, w_down)).reshape(peers, capacity, tile, channels)
    result = result * filled.astype(F32)[:, :, None, None]
    return result.astype(BF16).reshape(peers, pair, channels)


def per_device(
    atmosphere,
    conv_weight,
    atm_gain,
    atm_up,
    atm_down,
    flux_weight,
    land_mask,
    tile_owner,
    ocean_state,
    ocn_gain,
    ocn_up,
    ocn_down,
):
    margin = conv_weight.shape[0] // 2
    channels = atmosphere.shape[2]
    _, peers, capacity, tile, _ = ocean_state.shape
    pair = capacity * tile
    packed = -(-(pair * 13 // 16) // 8) * 8
    n_lon, n_lat = lax.axis_size("lon"), lax.axis_size("lat")
    owners = tile_owner.reshape(-1)
    state = ocean_state.reshape(peers, pair, channels)

    around = [(i, (i + 1) % n_lon) for i in range(n_lon)]
    left = lax.ppermute(atmosphere[:, -RIM:], "lon", around)
    right = lax.ppermute(atmosphere[:, :RIM], "lon", [(j, i) for i, j in around])
    mixed, own = conv_inner(atmosphere, conv_weight)
    up, down = widen(own, left, right, margin)
    north = [(i, i + 1) for i in range(n_lat - 1)]
    top = lax.ppermute(down, "lat", north)
    bottom = lax.ppermute(up, "lat", [(j, i) for i, j in north])
    mixed, w_up, w_down, w_flux = conv_outer(
        mixed, own, left, right, conv_weight, (atm_up, atm_down, flux_weight)
    )
    atm_out, packets, mark, _ = atmosphere_step(
        mixed, own, top, bottom, conv_weight, atm_gain, w_up, w_down, w_flux, owners,
        land_mask.reshape(owners.shape[0], tile), peers, capacity, tile, packed,
    )
    arrived = lax.all_to_all(packets, ("lat", "lon"), split_axis=0, concat_axis=0, tiled=True)
    near = fetch(mark, (state, ocn_gain.reshape(1, -1), ocn_up, ocn_down))
    ocean_out, over = ocean_step(near[0], arrived, *near[1:], capacity)
    ocean_out = lax.cond(
        over[0, 0] > 0,
        lambda packed_out: full_exchange(
            atm_out, flux_weight, land_mask, owners, state, ocn_gain, ocn_up, ocn_down, capacity
        ),
        lambda packed_out: packed_out,
        ocean_out,
    )
    return atm_out, ocean_out.reshape(ocean_state.shape)


def solution(mesh):
    placed = (
        P("lat", "lon", None),
        P(),
        P(),
        P(),
        P(),
        P(),
        P("lat", "lon"),
        P("lat", "lon", None),
        P(("lat", "lon"), None, None, None, None),
        P(),
        P(),
        P(),
    )
    return jax.shard_map(
        per_device,
        mesh=mesh,
        in_specs=placed,
        out_specs=(P("lat", "lon", None), P(("lat", "lon"), None, None, None, None)),
        check_vma=False,
    )
```

```python
import functools

import jax
import jax.numpy as jnp
from jax import lax
from jax.experimental import pallas as pl
from jax.experimental.pallas import tpu as pltpu
from jax.sharding import PartitionSpec as P

LANES = 128
SENDS = 8
RIM = 8
SIDE = 16
VMEM_BYTES = 48 << 20
F32, BF16 = jnp.float32, jnp.bfloat16
ANY = pl.BlockSpec(memory_space=pl.ANY)
IN_VMEM = pl.BlockSpec(memory_space=pltpu.VMEM)


def hbm(x):
    return pltpu.with_memory_space_constraint(x, pltpu.HBM)


def vmem(x):
    return pltpu.with_memory_space_constraint(x, pltpu.VMEM)


def dot(a, b):
    return jnp.dot(a, b, preferred_element_type=F32)


def iota(shape, dim):
    return lax.broadcasted_iota(jnp.int32, shape, dim)


def spread_weights(w_ref, wb, width):
    for h in range(wb.shape[0]):
        for p in range(width):
            for q in range(width):
                row = w_ref[p, q : q + 1, h * LANES : (h + 1) * LANES]
                wb[h, p * width + q] = jnp.broadcast_to(row, (8, LANES))


PRODUCTS = (
    ((0,), (4,)),
    ((1,), (5,)),
    ((0, 1), (4, 5)),
    ((0, 2), (4, 6)),
    ((1, 3), (5,)),
    ((0, 1, 2, 3), (4, 5, 6)),
    ((2,), (6,)),
    ((3,),),
    ((2, 3), (6,)),
)
WIDTH = 7
MARGIN = WIDTH // 2
TAPS = sum(len(p) for p in PRODUCTS)


def spread_products(w_ref, wb):
    for h in range(wb.shape[0]):
        at = 0
        for product in PRODUCTS:
            for q in range(WIDTH):
                for tap in product:
                    row = None
                    for p in tap:
                        one = w_ref[p, q : q + 1, h * LANES : (h + 1) * LANES]
                        row = one if row is None else row + one
                    wb[h, at] = jnp.broadcast_to(row, (8, LANES))
                    at += 1


def combine_rows(get, put, rows):
    blank = jnp.zeros_like(get(0))
    seen = {}

    def row(r):
        if r < 0 or r >= rows:
            return blank
        if r not in seen:
            seen[r] = get(r)
        return seen[r]

    for m in range(rows // 4 + 1):
        x = [row(4 * m + a - MARGIN) for a in range(WIDTH)]
        d0, d1, d2 = x[0] - x[2], x[1] - x[3], x[2] - x[4]
        e1, e2 = x[5] - x[3], x[6] - x[4]
        values = (d0 - d1, d2 - d1, d1, x[2] - x[3], x[4] - x[3], x[3], -d2 - e1, e2 - e1, e1)
        for k, value in enumerate(values):
            put(k, m, value)


GIVES = ((0,), (1,), (0, 1), (0, 2), (1, 3), (0, 1, 2, 3), (2,), (3,), (2, 3))


def filter_rows(read, wb, h, count):
    out = [None] * (4 * count)
    at = 0
    for k, product in enumerate(PRODUCTS):
        acc = [None] * count
        for q in range(WIDTH):
            window = [read(k, m, q) for m in range(count + len(product) - 1)]
            for t in range(len(product)):
                w = wb[h, at]
                at += 1
                for m in range(count):
                    term = window[m + t] * w
                    acc[m] = term if acc[m] is None else acc[m] + term
        for m in range(count):
            for i in GIVES[k]:
                before = out[4 * m + i]
                out[4 * m + i] = acc[m] if before is None else before + acc[m]
    return out


def edges_kernel(x_ref, w_ref, own_ref, kept_ref, first_ref, last_ref, sems):
    cols = own_ref.shape[1]
    copies = [
        pltpu.make_async_copy(x_ref, own_ref, sems.at[0]),
        pltpu.make_async_copy(w_ref, kept_ref, sems.at[1]),
    ]
    for copy in copies:
        copy.start()
    for copy in copies:
        copy.wait()
    first_ref[...] = own_ref[:, 0:RIM]
    last_ref[...] = own_ref[:, cols - RIM :]


def edges(atmosphere, conv_weight):
    rows, _, channels = atmosphere.shape
    return pl.pallas_call(
        edges_kernel,
        out_shape=[
            pltpu.VMEM(atmosphere.shape, BF16),
            pltpu.VMEM(conv_weight.shape, F32),
            pltpu.VMEM((rows, RIM, channels), BF16),
            pltpu.VMEM((rows, RIM, channels), BF16),
        ],
        in_specs=[ANY, ANY],
        out_specs=[IN_VMEM] * 4,
        scratch_shapes=[pltpu.SemaphoreType.DMA((2,))],
        compiler_params=pltpu.CompilerParams(vmem_limit_bytes=VMEM_BYTES),
        name="edges",
    )(hbm(atmosphere), hbm(conv_weight))


GROUP = 8


def inner_kernel(own_ref, w_ref, mixed_ref, wb, fs):
    rows, cols, channels = own_ref.shape
    spread_products(w_ref, wb)
    halves = channels // LANES
    first = SIDE - RIM
    for h in range(halves):
        part = slice(h * LANES, (h + 1) * LANES)

        def prepare(c, carry):
            c0 = pl.multiple_of(c * 16, 16)

            def put(k, m, value):
                fs[h, k, m, pl.ds(c0, 16)] = value

            combine_rows(lambda r: own_ref[r, pl.ds(c0 + first, 16), part].astype(F32), put, rows)
            return carry

        lax.fori_loop(0, fs.shape[3] // 16, prepare, 0)
    blocks = (cols - 2 * SIDE) // 8

    def body(step, carry):
        m0 = (step // blocks) * GROUP
        c0 = pl.multiple_of((step % blocks) * 8, 8)
        for h in range(halves):
            out = filter_rows(
                lambda k, m, q: fs[h, k, m0 + m, pl.ds(c0 + (RIM - MARGIN + q), 8)], wb, h, GROUP
            )
            for i, value in enumerate(out):
                mixed_ref[h, m0 * 4 + i, pl.ds(c0 + SIDE, 8)] = value
        return carry

    lax.fori_loop(0, (rows // 4 // GROUP) * blocks, body, 0)


def conv_inner(own, conv_weight):
    rows, cols, channels = own.shape
    halves = channels // LANES
    return pl.pallas_call(
        inner_kernel,
        out_shape=[
            pltpu.VMEM((halves, rows, cols, LANES), F32),
            pltpu.VMEM((halves, WIDTH * TAPS, 8, LANES), F32),
        ],
        in_specs=[IN_VMEM, IN_VMEM],
        out_specs=[IN_VMEM, IN_VMEM],
        scratch_shapes=[
            pltpu.VMEM((halves, len(PRODUCTS), rows // 4 + 1, cols - 2 * (SIDE - RIM), LANES), F32),
        ],
        compiler_params=pltpu.CompilerParams(vmem_limit_bytes=VMEM_BYTES),
        cost_estimate=pl.CostEstimate(
            flops=2 * rows * cols * channels * WIDTH * WIDTH, bytes_accessed=6 * rows * cols * channels, transcendentals=0
        ),
        name="conv_inner",
    )(vmem(own), vmem(conv_weight))


def outer_kernel(mixed_in, own_ref, left_ref, right_ref, wb, *refs, count):
    far, mixed_ref, near = refs[:count], refs[count], refs[count + 1 : 2 * count + 1]
    fs, sems = refs[2 * count + 1 :]
    fetches = [pltpu.make_async_copy(f, n, sems.at[i]) for i, (f, n) in enumerate(zip(far, near))]
    for fetch in fetches:
        fetch.start()
    rows, cols, channels = own_ref.shape
    halves = channels // LANES
    blocks = SIDE // 8
    for side in range(2):
        rim, edge = (left_ref, 0) if side == 0 else (right_ref, SIDE + RIM)
        body_at, own_at = (RIM, 0) if side == 0 else (0, cols - SIDE - RIM)
        for h in range(halves):
            part = slice(h * LANES, (h + 1) * LANES)

            def put_rim(k, m, value):
                fs[k, m, edge : edge + RIM] = value

            combine_rows(lambda r: rim[r, :, part].astype(F32), put_rim, rows)

            def prepare(c, carry):
                c0 = pl.multiple_of(c * 8, 8)

                def put(k, m, value):
                    fs[k, m, pl.ds(c0 + body_at, 8)] = value

                combine_rows(lambda r: own_ref[r, pl.ds(c0 + own_at, 8), part].astype(F32), put, rows)
                return carry

            lax.fori_loop(0, blocks + 1, prepare, 0)

            def body(step, carry):
                m0 = (step // blocks) * GROUP
                c0 = pl.multiple_of((step % blocks) * 8, 8)
                out = filter_rows(
                    lambda k, m, q: fs[k, m0 + m, pl.ds(c0 + (RIM - MARGIN + q), 8)], wb, h, GROUP
                )
                for i, value in enumerate(out):
                    mixed_ref[h, m0 * 4 + i, pl.ds(c0 + side * (cols - SIDE), 8)] = value
                return carry

            lax.fori_loop(0, (rows // 4 // GROUP) * blocks, body, 0)
    for fetch in fetches:
        fetch.wait()


def conv_outer(mixed, own, left, right, products, weights):
    rows, cols, channels = own.shape
    halves = channels // LANES
    count = len(weights)
    return pl.pallas_call(
        functools.partial(outer_kernel, count=count),
        out_shape=[pltpu.VMEM(mixed.shape, F32)] + [pltpu.VMEM(w.shape, w.dtype) for w in weights],
        in_specs=[IN_VMEM] * 5 + [ANY] * count,
        out_specs=[IN_VMEM] * (count + 1),
        input_output_aliases={0: 0},
        scratch_shapes=[
            pltpu.VMEM((len(PRODUCTS), rows // 4 + 1, SIDE + 2 * RIM, LANES), F32),
            pltpu.SemaphoreType.DMA((count,)),
        ],
        compiler_params=pltpu.CompilerParams(vmem_limit_bytes=VMEM_BYTES),
        cost_estimate=pl.CostEstimate(
            flops=4 * rows * RIM * channels * WIDTH * WIDTH, bytes_accessed=12 * rows * RIM * channels, transcendentals=0
        ),
        name="conv_outer",
    )(vmem(mixed), vmem(own), vmem(left), vmem(right), vmem(products), *[hbm(w) for w in weights])


def widen_kernel(own_ref, left_ref, right_ref, mixed_ref, up_ref, down_ref):
    margin = up_ref.shape[0]
    rows, cols, _ = own_ref.shape
    for out, at in ((up_ref, 0), (down_ref, rows - margin)):
        out[:, 0:RIM] = left_ref[at : at + margin]
        out[:, RIM : RIM + cols] = own_ref[at : at + margin]
        out[:, RIM + cols :] = right_ref[at : at + margin]


def widen(own, left, right, mixed, margin):
    rows, cols, channels = own.shape
    return pl.pallas_call(
        widen_kernel,
        out_shape=[pltpu.VMEM((margin, cols + 2 * RIM, channels), BF16)] * 2,
        in_specs=[IN_VMEM] * 4,
        out_specs=[IN_VMEM] * 2,
        compiler_params=pltpu.CompilerParams(vmem_limit_bytes=VMEM_BYTES),
        name="widen_rows",
    )(vmem(own), vmem(left), vmem(right), vmem(mixed))


def normalize(values, gain):
    average = jnp.mean(values, axis=-1, keepdims=True)
    centred = values - average
    spread = jnp.mean(centred * centred, axis=-1, keepdims=True)
    return (centred * lax.rsqrt(spread + 1e-06) * gain).astype(BF16)


def mixer(normed, up_ref, down_ref, chunk=256):
    c0 = 0.7978845608028654
    c1 = c0 * 0.044715
    total = None
    for j in range(0, up_ref.shape[1], chunk):
        x = dot(normed, up_ref[:, j : j + chunk])
        gate = jnp.tanh(x * (c0 + c1 * (x * x)))
        hidden = (x + x * gate).astype(BF16)
        part = dot(hidden, down_ref[j : j + chunk, :])
        total = part if total is None else total + part
    return 0.5 * total


def atmosphere_kernel(
    tiles, capacity, tile, owner_sm, mixed_in, atm_ref, top_ref, bottom_ref, w_ref, gain_ref, up_ref, down_ref,
    flux_ref, owner_ref, mask_ref, out_ref, send_ref, rest_ref, mark_ref, mixed_ref,
    wb, strip, fluxes, order_sm, meta, places, new_out, packets, rest, out_sems, send_sems, rest_sems,
):
    rows, cols, channels = atm_ref.shape
    width = w_ref.shape[0]
    margin = width // 2
    halves = channels // LANES
    peers, packed, _ = send_ref.shape
    pair = capacity * tile

    def lanes(h):
        return slice(h * LANES, (h + 1) * LANES)

    spread_weights(w_ref, wb, width)

    def latitude(rows_ref, pairs):
        for h in range(halves):
            strip[h] = rows_ref[:, :, lanes(h)].astype(F32)

        def body(c, carry):
            c0 = pl.multiple_of(c * 8, 8)
            for h in range(halves):
                for i, taps in pairs:
                    acc = mixed_ref[h, i, pl.ds(c0, 8)]
                    for row, p in taps:
                        for q in range(width):
                            acc += strip[h, row, pl.ds(c0 + (RIM - margin + q), 8)] * wb[h, p * width + q]
                    mixed_ref[h, i, pl.ds(c0, 8)] = acc
            return carry

        lax.fori_loop(0, cols // 8, body, 0)

    latitude(top_ref, [(i, [(i + p, p) for p in range(margin - i)]) for i in range(margin)])
    latitude(
        bottom_ref,
        [
            (rows - margin + i, [(i - e, width - 1 - e) for e in range(i + 1)])
            for i in range(margin)
        ],
    )

    block = 16
    cells = block * cols

    def leave(step):
        part = pl.ds(step * block, block)
        return pltpu.make_async_copy(new_out.at[part], out_ref.at[part], out_sems.at[step])

    def mix(step, carry):
        r0 = step * block
        parts = [mixed_ref[h, pl.ds(r0, block)].reshape(cells, LANES) for h in range(halves)]
        normed = normalize(jnp.concatenate(parts, axis=1), gain_ref[...])
        branch = mixer(normed, up_ref, down_ref)
        new = (atm_ref[pl.ds(r0, block)].reshape(cells, channels).astype(F32) + branch).astype(BF16)
        new_out[pl.ds(r0, block)] = new.reshape(block, cols, channels)
        leave(step).start()
        fluxes[pl.ds(pl.multiple_of(step * cells, cells), cells), :] = dot(new, flux_ref[...]).astype(BF16)
        return carry

    lax.fori_loop(0, rows // block, mix, 0)

    member = (owner_ref[...] == iota((peers, tiles), 0)).astype(F32)
    before = (iota((tiles, tiles), 0) < iota((tiles, tiles), 1)).astype(BF16)
    rank = dot(member.astype(BF16), before)
    bits = jnp.zeros((peers, LANES), F32)
    flags = jnp.zeros((peers, LANES), F32)
    lane = iota((peers, LANES), 1)
    for r in range(capacity):
        chosen = jnp.where(rank == float(r), member, 0.0)
        at = (iota((tile, LANES), 1) == iota((tile, LANES), 0) + r * tile).astype(BF16)
        shifted = dot(mask_ref[...].astype(F32).astype(BF16), at).astype(BF16)
        bits += dot(chosen.astype(BF16), shifted)
        flags += jnp.where(lane == r, jnp.sum(chosen, axis=1, keepdims=True), 0.0)
    over = jnp.max(jnp.sum(bits, axis=1, keepdims=True), axis=0, keepdims=True) > float(packed - 1)
    flags += jnp.where((lane == capacity) & over, 1.0, 0.0)
    meta[:, 0:LANES] = bits
    meta[:, LANES:] = flags
    ahead = jnp.where(
        iota((LANES, LANES), 0) < iota((LANES, LANES), 1),
        1.0,
        jnp.where(iota((LANES, LANES), 0) == iota((LANES, LANES), 1), 1000.0, 0.0),
    ).astype(BF16)
    places[...] = (dot(bits.astype(BF16), ahead) - 999.0).astype(jnp.int32)

    def clear(o, carry):
        for r in range(capacity):
            order_sm[o * capacity + r] = 0
        order_sm[peers * capacity + o] = 0
        return carry

    lax.fori_loop(0, peers, clear, 0)

    def count(t, carry):
        o = owner_sm[t]
        r = order_sm[peers * capacity + o]
        order_sm[o * capacity + r] = t
        order_sm[peers * capacity + o] = r + 1
        return carry

    lax.fori_loop(0, tiles, count, 0)
    order = iota((packed + rest_ref.shape[1], LANES), 0)
    top_row = iota((packed, channels), 0) == 0
    group = peers // SENDS

    def send(i):
        part = pl.ds(i * group, group)
        return (
            pltpu.make_async_copy(packets.at[part], send_ref.at[part], send_sems.at[i]),
            pltpu.make_async_copy(rest.at[part], rest_ref.at[part], rest_sems.at[i]),
        )

    def pack(i, carry):
        for k in range(group):
            o = i * group + k
            held = [
                fluxes[pl.ds(pl.multiple_of(order_sm[o * capacity + r] * tile, tile), tile), :]
                for r in range(capacity)
            ]
            pick = jnp.where(order == places[pl.ds(o, 1), :], 1.0, 0.0).astype(BF16)
            packet = dot(pick[:, 0:pair], jnp.concatenate(held, axis=0))
            packets[o] = jnp.where(top_row, meta[pl.ds(o, 1), :], packet[0:packed]).astype(BF16)
            rest[o] = packet[packed:].astype(BF16)
        for copy in send(i):
            copy.start()
        return carry

    lax.fori_loop(0, SENDS, pack, 0)
    mark_ref[...] = jnp.zeros(mark_ref.shape, F32)
    for step in range(rows // block):
        leave(step).wait()
    for i in range(SENDS):
        for copy in send(i):
            copy.wait()


def atmosphere_step(
    mixed, own, top, bottom, conv_weight, gain, w_up, w_down, w_flux, owners, mask, peers, capacity, tile, packed
):
    rows, cols, channels = own.shape
    tiles = owners.shape[0]
    width = conv_weight.shape[0]
    margin = width // 2
    halves = channels // LANES
    hidden = w_up.shape[1]
    cells = rows * cols
    remaining = -(-(capacity * tile + 1 - packed) // 16) * 16
    in_smem = pl.BlockSpec(memory_space=pltpu.SMEM)
    return pl.pallas_call(
        functools.partial(atmosphere_kernel, tiles, capacity, tile),
        out_shape=[
            jax.ShapeDtypeStruct((rows, cols, channels), BF16),
            jax.ShapeDtypeStruct((peers, packed, channels), BF16),
            jax.ShapeDtypeStruct((peers, remaining, channels), BF16),
            jax.ShapeDtypeStruct((8, LANES), F32),
            pltpu.VMEM(mixed.shape, F32),
        ],
        in_specs=[in_smem] + [IN_VMEM] * 11,
        out_specs=[ANY, ANY, ANY, IN_VMEM, IN_VMEM],
        input_output_aliases={1: 4},
        scratch_shapes=[
            pltpu.VMEM((halves, width * width, 8, LANES), F32),
            pltpu.VMEM((halves, margin, cols + 2 * RIM, LANES), F32),
            pltpu.VMEM((cells, channels), BF16),
            pltpu.SMEM((peers * (capacity + 1),), jnp.int32),
            pltpu.VMEM((peers, 2 * LANES), F32),
            pltpu.VMEM((peers, LANES), jnp.int32),
            pltpu.VMEM((rows, cols, channels), BF16),
            pltpu.VMEM((peers, packed, channels), BF16),
            pltpu.VMEM((peers, remaining, channels), BF16),
            pltpu.SemaphoreType.DMA((rows,)),
            pltpu.SemaphoreType.DMA((SENDS,)),
            pltpu.SemaphoreType.DMA((SENDS,)),
        ],
        compiler_params=pltpu.CompilerParams(vmem_limit_bytes=VMEM_BYTES),
        cost_estimate=pl.CostEstimate(
            flops=2 * cells * channels * (2 * hidden + channels), bytes_accessed=12 * cells * channels,
            transcendentals=cells * hidden,
        ),
        name="atmosphere",
    )(
        owners, vmem(mixed), vmem(own), vmem(top), vmem(bottom), vmem(conv_weight), gain.reshape(1, -1), vmem(w_up),
        vmem(w_down), vmem(w_flux), owners.reshape(1, -1), mask,
    )


def fetch_kernel(mark_ref, *refs):
    count = (len(refs) - 1) // 2
    copies = [
        pltpu.make_async_copy(refs[i], refs[count + i], refs[-1].at[i]) for i in range(count)
    ]
    for copy in copies:
        copy.start()
    for copy in copies:
        copy.wait()


def fetch(mark, arrays):
    return pl.pallas_call(
        fetch_kernel,
        out_shape=[pltpu.VMEM(x.shape, x.dtype) for x in arrays],
        in_specs=[ANY] * (len(arrays) + 1),
        out_specs=[IN_VMEM] * len(arrays),
        scratch_shapes=[pltpu.SemaphoreType.DMA((len(arrays),))],
        compiler_params=pltpu.CompilerParams(vmem_limit_bytes=VMEM_BYTES),
        name="fetch",
    )(mark, *[hbm(x) for x in arrays])


def ocean_kernel(
    capacity, chain, state_ref, packet_hbm, gain_ref, up_ref, down_ref, out_hbm, over_ref, packet_ref, out_ref,
    in_sems, out_sems,
):
    peers, pair, channels = state_ref.shape
    packed = packet_ref.shape[1]
    tile = pair // capacity
    chains = peers // chain

    def arrive(i):
        part = pl.ds(i * chain, chain)
        return pltpu.make_async_copy(packet_hbm.at[part], packet_ref.at[part], in_sems.at[i])

    def leave(i):
        part = pl.ds(i * chain, chain)
        return pltpu.make_async_copy(out_ref.at[part], out_hbm.at[part], out_sems.at[i])

    for i in range(chains):
        arrive(i).start()
    ahead = jnp.where(
        iota((pair, LANES), 1) < iota((pair, LANES), 0),
        1.0,
        jnp.where(iota((pair, LANES), 1) == iota((pair, LANES), 0), 1000.0, 0.0),
    ).astype(BF16)
    order = iota((pair, packed), 1)

    def mix(i, over):
        arrive(i).wait()
        first = i * chain
        head = jnp.concatenate([packet_ref[first + g, 0:1, :] for g in range(chain)], axis=0)
        place = lax.dot_general(
            ahead, head[:, 0:LANES], (((1,), (1,)), ((), ())), preferred_element_type=F32
        )
        place = (place - 999.0).astype(jnp.int32)
        flags = head[:, LANES:].astype(F32)
        states = []
        for g in range(chain):
            pick = jnp.where(order == place[:, g : g + 1], 1.0, 0.0).astype(BF16)
            states.append(state_ref[first + g].astype(F32) + dot(pick, packet_ref[first + g]))
        states = jnp.concatenate(states, axis=0)
        result = states + mixer(normalize(states, gain_ref[...]), up_ref, down_ref)
        for g in range(chain):
            for r in range(capacity):
                used = flags[g : g + 1, r : r + 1] > 0.0
                at = g * pair + r * tile
                part = jnp.where(used, result[at : at + tile], 0.0)
                out_ref[first + g, r * tile : (r + 1) * tile, :] = part.astype(BF16)
        leave(i).start()
        return jnp.maximum(over, jnp.max(flags[:, capacity : capacity + 1], axis=0, keepdims=True))

    over = lax.fori_loop(0, chains, mix, jnp.zeros((1, 1), F32))
    over_ref[0, 0] = jnp.max(over)
    for i in range(chains):
        leave(i).wait()


def ocean_step(state, packets, gain, w_up, w_down, capacity):
    peers, pair, channels = state.shape
    packed = packets.shape[1]
    hidden = w_up.shape[1]
    chain = min(peers, 1024 // pair)
    chains = peers // chain
    cells = peers * pair
    return pl.pallas_call(
        functools.partial(ocean_kernel, capacity, chain),
        out_shape=[
            jax.ShapeDtypeStruct((peers, pair, channels), BF16),
            jax.ShapeDtypeStruct((1, 1), F32),
        ],
        in_specs=[IN_VMEM, ANY, IN_VMEM, IN_VMEM, IN_VMEM],
        out_specs=[ANY, pl.BlockSpec(memory_space=pltpu.SMEM)],
        scratch_shapes=[
            pltpu.VMEM((peers, packed, channels), BF16),
            pltpu.VMEM((peers, pair, channels), BF16),
            pltpu.SemaphoreType.DMA((chains,)),
            pltpu.SemaphoreType.DMA((chains,)),
        ],
        compiler_params=pltpu.CompilerParams(vmem_limit_bytes=VMEM_BYTES),
        cost_estimate=pl.CostEstimate(
            flops=4 * cells * channels * hidden, bytes_accessed=6 * cells * channels, transcendentals=cells * hidden
        ),
        name="ocean",
    )(vmem(state), hbm(packets), gain, vmem(w_up), vmem(w_down))


def per_device(
    atmosphere,
    conv_weight,
    atm_gain,
    atm_up,
    atm_down,
    flux_weight,
    land_mask,
    tile_owner,
    ocean_state,
    ocn_gain,
    ocn_up,
    ocn_down,
):
    margin = conv_weight.shape[0] // 2
    channels = atmosphere.shape[2]
    _, peers, capacity, tile, _ = ocean_state.shape
    pair = capacity * tile
    packed = -(-(pair * 13 // 16) // 8) * 8
    n_lon, n_lat = lax.axis_size("lon"), lax.axis_size("lat")
    owners = tile_owner.reshape(-1)
    state = ocean_state.reshape(peers, pair, channels)

    around = [(i, (i + 1) % n_lon) for i in range(n_lon)]
    own, conv_weight, first, last = edges(atmosphere, conv_weight)
    left = lax.ppermute(last, "lon", around)
    right = lax.ppermute(first, "lon", [(j, i) for i, j in around])
    mixed, products = conv_inner(own, conv_weight)
    up, down = widen(own, left, right, mixed, margin)
    north = [(i, i + 1) for i in range(n_lat - 1)]
    top = lax.ppermute(down, "lat", north)
    bottom = lax.ppermute(up, "lat", [(j, i) for i, j in north])
    mixed, w_up, w_down, w_flux = conv_outer(
        mixed, own, left, right, products, (atm_up, atm_down, flux_weight)
    )
    atm_out, packets, rest, mark, _ = atmosphere_step(
        mixed, own, top, bottom, conv_weight, atm_gain, w_up, w_down, w_flux, owners,
        land_mask.reshape(owners.shape[0], tile), peers, capacity, tile, packed,
    )

    def exchange(x):
        return lax.all_to_all(x, ("lat", "lon"), split_axis=0, concat_axis=0, tiled=True)

    arrived = exchange(packets)
    near = fetch(mark, (state, ocn_gain.reshape(1, -1), ocn_up, ocn_down))
    ocean_out, over = ocean_step(near[0], arrived, *near[1:], capacity)

    def with_rest(packed_out):
        everything = jnp.concatenate([arrived, exchange(rest)], axis=1)
        return ocean_step(near[0], everything, *near[1:], capacity)[0]

    ocean_out = lax.cond(over[0, 0] > 0, with_rest, lambda packed_out: packed_out, ocean_out)
    return atm_out, ocean_out.reshape(ocean_state.shape)


def solution(mesh):
    placed = (
        P("lat", "lon", None),
        P(),
        P(),
        P(),
        P(),
        P(),
        P("lat", "lon"),
        P("lat", "lon", None),
        P(("lat", "lon"), None, None, None, None),
        P(),
        P(),
        P(),
    )
    return jax.shard_map(
        per_device,
        mesh=mesh,
        in_specs=placed,
        out_specs=(P("lat", "lon", None), P(("lat", "lon"), None, None, None, None)),
        check_vma=False,
    )
```

```python
import functools

import jax
import jax.numpy as jnp
from jax import lax
from jax.experimental import pallas as pl
from jax.experimental.pallas import tpu as pltpu
from jax.sharding import PartitionSpec as P

LANES = 128
SENDS = 2
RIM = 8
SIDE = 16
VMEM_BYTES = 48 << 20
F32, BF16 = jnp.float32, jnp.bfloat16
ANY = pl.BlockSpec(memory_space=pl.ANY)
IN_VMEM = pl.BlockSpec(memory_space=pltpu.VMEM)
IN_SMEM = pl.BlockSpec(memory_space=pltpu.SMEM)


def hbm(x):
    return pltpu.with_memory_space_constraint(x, pltpu.HBM)


def vmem(x):
    return pltpu.with_memory_space_constraint(x, pltpu.VMEM)


def dot(a, b):
    return jnp.dot(a, b, preferred_element_type=F32)


def iota(shape, dim):
    return lax.broadcasted_iota(jnp.int32, shape, dim)


def spread_weights(w_ref, wb, width):
    for h in range(wb.shape[0]):
        for p in range(width):
            for q in range(width):
                row = w_ref[p, q : q + 1, h * LANES : (h + 1) * LANES]
                wb[h, p * width + q] = jnp.broadcast_to(row, (8, LANES))


PRODUCTS = (
    ((0,), (4,)),
    ((1,), (5,)),
    ((0, 1), (4, 5)),
    ((0, 2), (4, 6)),
    ((1, 3), (5,)),
    ((0, 1, 2, 3), (4, 5, 6)),
    ((2,), (6,)),
    ((3,),),
    ((2, 3), (6,)),
)
WIDTH = 7
MARGIN = WIDTH // 2
TAPS = sum(len(p) for p in PRODUCTS)


def spread_products(w_ref, wb):
    for h in range(wb.shape[0]):
        at = 0
        for product in PRODUCTS:
            for q in range(WIDTH):
                for tap in product:
                    row = None
                    for p in tap:
                        one = w_ref[p, q : q + 1, h * LANES : (h + 1) * LANES]
                        row = one if row is None else row + one
                    wb[h, at] = jnp.broadcast_to(row, (8, LANES))
                    at += 1


def combine_rows(get, put, rows):
    blank = jnp.zeros_like(get(0))
    seen = {}

    def row(r):
        if r < 0 or r >= rows:
            return blank
        if r not in seen:
            seen[r] = get(r)
        return seen[r]

    for m in range(rows // 4 + 1):
        x = [row(4 * m + a - MARGIN) for a in range(WIDTH)]
        d0, d1, d2 = x[0] - x[2], x[1] - x[3], x[2] - x[4]
        e1, e2 = x[5] - x[3], x[6] - x[4]
        values = (d0 - d1, d2 - d1, d1, x[2] - x[3], x[4] - x[3], x[3], -d2 - e1, e2 - e1, e1)
        for k, value in enumerate(values):
            put(k, m, value)


GIVES = ((0,), (1,), (0, 1), (0, 2), (1, 3), (0, 1, 2, 3), (2,), (3,), (2, 3))


def filter_rows(read, wb, h, count):
    out = [None] * (4 * count)
    at = 0
    for k, product in enumerate(PRODUCTS):
        acc = [None] * count
        for q in range(WIDTH):
            window = [read(k, m, q) for m in range(count + len(product) - 1)]
            for t in range(len(product)):
                w = wb[h, at]
                at += 1
                for m in range(count):
                    term = window[m + t] * w
                    acc[m] = term if acc[m] is None else acc[m] + term
        for m in range(count):
            for i in GIVES[k]:
                before = out[4 * m + i]
                out[4 * m + i] = acc[m] if before is None else before + acc[m]
    return out


def edges_kernel(x_ref, w_ref, own_ref, kept_ref, first_ref, last_ref, sems):
    cols = own_ref.shape[1]
    copies = [
        pltpu.make_async_copy(x_ref, own_ref, sems.at[0]),
        pltpu.make_async_copy(w_ref, kept_ref, sems.at[1]),
    ]
    for copy in copies:
        copy.start()
    for copy in copies:
        copy.wait()
    first_ref[...] = own_ref[:, 0:RIM]
    last_ref[...] = own_ref[:, cols - RIM :]


def edges(atmosphere, conv_weight):
    rows, _, channels = atmosphere.shape
    return pl.pallas_call(
        edges_kernel,
        out_shape=[
            pltpu.VMEM(atmosphere.shape, BF16),
            pltpu.VMEM(conv_weight.shape, F32),
            pltpu.VMEM((rows, RIM, channels), BF16),
            pltpu.VMEM((rows, RIM, channels), BF16),
        ],
        in_specs=[ANY, ANY],
        out_specs=[IN_VMEM] * 4,
        scratch_shapes=[pltpu.SemaphoreType.DMA((2,))],
        compiler_params=pltpu.CompilerParams(vmem_limit_bytes=VMEM_BYTES),
        name="edges",
    )(hbm(atmosphere), hbm(conv_weight))


GROUP = 8


def inner_kernel(own_ref, w_ref, mixed_ref, wb, fs):
    rows, cols, channels = own_ref.shape
    spread_products(w_ref, wb)
    halves = channels // LANES
    first = SIDE - RIM
    for h in range(halves):
        part = slice(h * LANES, (h + 1) * LANES)

        def prepare(c, carry):
            c0 = pl.multiple_of(c * 16, 16)

            def put(k, m, value):
                fs[h, k, m, pl.ds(c0, 16)] = value

            combine_rows(lambda r: own_ref[r, pl.ds(c0 + first, 16), part].astype(F32), put, rows)
            return carry

        lax.fori_loop(0, fs.shape[3] // 16, prepare, 0)
    blocks = (cols - 2 * SIDE) // 8

    def body(step, carry):
        m0 = (step // blocks) * GROUP
        c0 = pl.multiple_of((step % blocks) * 8, 8)
        for h in range(halves):
            out = filter_rows(
                lambda k, m, q: fs[h, k, m0 + m, pl.ds(c0 + (RIM - MARGIN + q), 8)], wb, h, GROUP
            )
            for i, value in enumerate(out):
                mixed_ref[h, m0 * 4 + i, pl.ds(c0 + SIDE, 8)] = value
        return carry

    lax.fori_loop(0, (rows // 4 // GROUP) * blocks, body, 0)


def conv_inner(own, conv_weight):
    rows, cols, channels = own.shape
    halves = channels // LANES
    return pl.pallas_call(
        inner_kernel,
        out_shape=[
            pltpu.VMEM((halves, rows, cols, LANES), F32),
            pltpu.VMEM((halves, WIDTH * TAPS, 8, LANES), F32),
        ],
        in_specs=[IN_VMEM, IN_VMEM],
        out_specs=[IN_VMEM, IN_VMEM],
        scratch_shapes=[
            pltpu.VMEM((halves, len(PRODUCTS), rows // 4 + 1, cols - 2 * (SIDE - RIM), LANES), F32),
        ],
        compiler_params=pltpu.CompilerParams(vmem_limit_bytes=VMEM_BYTES),
        cost_estimate=pl.CostEstimate(
            flops=2 * rows * cols * channels * WIDTH * WIDTH, bytes_accessed=6 * rows * cols * channels, transcendentals=0
        ),
        name="conv_inner",
    )(vmem(own), vmem(conv_weight))


def outer_kernel(mixed_in, own_ref, left_ref, right_ref, wb, *refs, count):
    far, mixed_ref, near = refs[:count], refs[count], refs[count + 1 : 2 * count + 1]
    fs, sems = refs[2 * count + 1 :]
    fetches = [pltpu.make_async_copy(f, n, sems.at[i]) for i, (f, n) in enumerate(zip(far, near))]
    for fetch in fetches:
        fetch.start()
    rows, cols, channels = own_ref.shape
    halves = channels // LANES
    blocks = SIDE // 8
    for side in range(2):
        rim, edge = (left_ref, 0) if side == 0 else (right_ref, SIDE + RIM)
        body_at, own_at = (RIM, 0) if side == 0 else (0, cols - SIDE - RIM)
        for h in range(halves):
            part = slice(h * LANES, (h + 1) * LANES)

            def put_rim(k, m, value):
                fs[k, m, edge : edge + RIM] = value

            combine_rows(lambda r: rim[r, :, part].astype(F32), put_rim, rows)

            def prepare(c, carry):
                c0 = pl.multiple_of(c * 8, 8)

                def put(k, m, value):
                    fs[k, m, pl.ds(c0 + body_at, 8)] = value

                combine_rows(lambda r: own_ref[r, pl.ds(c0 + own_at, 8), part].astype(F32), put, rows)
                return carry

            lax.fori_loop(0, blocks + 1, prepare, 0)

            def body(step, carry):
                m0 = (step // blocks) * GROUP
                c0 = pl.multiple_of((step % blocks) * 8, 8)
                out = filter_rows(
                    lambda k, m, q: fs[k, m0 + m, pl.ds(c0 + (RIM - MARGIN + q), 8)], wb, h, GROUP
                )
                for i, value in enumerate(out):
                    mixed_ref[h, m0 * 4 + i, pl.ds(c0 + side * (cols - SIDE), 8)] = value
                return carry

            lax.fori_loop(0, (rows // 4 // GROUP) * blocks, body, 0)
    for fetch in fetches:
        fetch.wait()


def conv_outer(mixed, own, left, right, products, weights):
    rows, cols, channels = own.shape
    halves = channels // LANES
    count = len(weights)
    return pl.pallas_call(
        functools.partial(outer_kernel, count=count),
        out_shape=[pltpu.VMEM(mixed.shape, F32)] + [pltpu.VMEM(w.shape, w.dtype) for w in weights],
        in_specs=[IN_VMEM] * 5 + [ANY] * count,
        out_specs=[IN_VMEM] * (count + 1),
        input_output_aliases={0: 0},
        scratch_shapes=[
            pltpu.VMEM((len(PRODUCTS), rows // 4 + 1, SIDE + 2 * RIM, LANES), F32),
            pltpu.SemaphoreType.DMA((count,)),
        ],
        compiler_params=pltpu.CompilerParams(vmem_limit_bytes=VMEM_BYTES),
        cost_estimate=pl.CostEstimate(
            flops=4 * rows * RIM * channels * WIDTH * WIDTH, bytes_accessed=12 * rows * RIM * channels, transcendentals=0
        ),
        name="conv_outer",
    )(vmem(mixed), vmem(own), vmem(left), vmem(right), vmem(products), *[hbm(w) for w in weights])


def widen_kernel(own_ref, left_ref, right_ref, mixed_ref, up_ref, down_ref):
    margin = up_ref.shape[0]
    rows, cols, _ = own_ref.shape
    for out, at in ((up_ref, 0), (down_ref, rows - margin)):
        out[:, 0:RIM] = left_ref[at : at + margin]
        out[:, RIM : RIM + cols] = own_ref[at : at + margin]
        out[:, RIM + cols :] = right_ref[at : at + margin]


def widen(own, left, right, mixed, margin):
    rows, cols, channels = own.shape
    return pl.pallas_call(
        widen_kernel,
        out_shape=[pltpu.VMEM((margin, cols + 2 * RIM, channels), BF16)] * 2,
        in_specs=[IN_VMEM] * 4,
        out_specs=[IN_VMEM] * 2,
        compiler_params=pltpu.CompilerParams(vmem_limit_bytes=VMEM_BYTES),
        name="widen_rows",
    )(vmem(own), vmem(left), vmem(right), vmem(mixed))


def normalize(values, gain):
    average = jnp.mean(values, axis=-1, keepdims=True)
    centred = values - average
    spread = jnp.mean(centred * centred, axis=-1, keepdims=True)
    return (centred * lax.rsqrt(spread + 1e-06) * gain).astype(BF16)


def mixer(normed, up_ref, down_ref, chunk=256):
    c0 = 0.7978845608028654
    c1 = c0 * 0.044715
    total = None
    for j in range(0, up_ref.shape[1], chunk):
        x = dot(normed, up_ref[:, j : j + chunk])
        gate = jnp.tanh(x * (c0 + c1 * (x * x)))
        hidden = (x + x * gate).astype(BF16)
        part = dot(hidden, down_ref[j : j + chunk, :])
        total = part if total is None else total + part
    return 0.5 * total


def atmosphere_kernel(
    tiles, capacity, tile, owner_sm, mixed_in, atm_ref, top_ref, bottom_ref, w_ref, gain_ref, up_ref, down_ref,
    flux_ref, owner_ref, mask_ref, out_ref, send_ref, rest_ref, mark_ref, mixed_ref,
    wb, strip, fluxes, order_sm, count_sm, meta, places, new_out, packets, rest, out_sems, send_sems, rest_sems,
):
    rows, cols, channels = atm_ref.shape
    width = w_ref.shape[0]
    margin = width // 2
    halves = channels // LANES
    peers, packed, _ = send_ref.shape
    pair = capacity * tile

    def lanes(h):
        return slice(h * LANES, (h + 1) * LANES)

    spread_weights(w_ref, wb, width)

    def latitude(rows_ref, pairs):
        for h in range(halves):
            strip[h] = rows_ref[:, :, lanes(h)].astype(F32)

        def body(c, carry):
            c0 = pl.multiple_of(c * 8, 8)
            for h in range(halves):
                for i, taps in pairs:
                    acc = mixed_ref[h, i, pl.ds(c0, 8)]
                    for row, p in taps:
                        for q in range(width):
                            acc += strip[h, row, pl.ds(c0 + (RIM - margin + q), 8)] * wb[h, p * width + q]
                    mixed_ref[h, i, pl.ds(c0, 8)] = acc
            return carry

        lax.fori_loop(0, cols // 8, body, 0)

    latitude(top_ref, [(i, [(i + p, p) for p in range(margin - i)]) for i in range(margin)])
    latitude(
        bottom_ref,
        [
            (rows - margin + i, [(i - e, width - 1 - e) for e in range(i + 1)])
            for i in range(margin)
        ],
    )

    block = rows
    cells = block * cols

    def leave(step):
        part = pl.ds(step * block, block)
        return pltpu.make_async_copy(new_out.at[part], out_ref.at[part], out_sems.at[step])

    def mix(step, carry):
        r0 = step * block
        parts = [mixed_ref[h, pl.ds(r0, block)].reshape(cells, LANES) for h in range(halves)]
        normed = normalize(jnp.concatenate(parts, axis=1), gain_ref[...])
        branch = mixer(normed, up_ref, down_ref)
        new = (atm_ref[pl.ds(r0, block)].reshape(cells, channels).astype(F32) + branch).astype(BF16)
        new_out[pl.ds(r0, block)] = new.reshape(block, cols, channels)
        leave(step).start()
        fluxes[pl.ds(pl.multiple_of(step * cells, cells), cells), :] = dot(new, flux_ref[...]).astype(BF16)
        return carry

    lax.fori_loop(0, rows // block, mix, 0)

    member = (owner_ref[...] == iota((peers, tiles), 0)).astype(F32)
    before = (iota((tiles, tiles), 0) < iota((tiles, tiles), 1)).astype(BF16)
    rank = dot(member.astype(BF16), before)
    bits = jnp.zeros((peers, LANES), F32)
    flags = jnp.zeros((peers, LANES), F32)
    lane = iota((peers, LANES), 1)
    for r in range(capacity):
        chosen = jnp.where(rank == float(r), member, 0.0)
        at = (iota((tile, LANES), 1) == iota((tile, LANES), 0) + r * tile).astype(BF16)
        shifted = dot(mask_ref[...].astype(F32).astype(BF16), at).astype(BF16)
        bits += dot(chosen.astype(BF16), shifted)
        flags += jnp.where(lane == r, jnp.sum(chosen, axis=1, keepdims=True), 0.0)
    over = jnp.max(jnp.sum(bits, axis=1, keepdims=True), axis=0, keepdims=True) > float(packed - 1)
    flags += jnp.where((lane == capacity) & over, 1.0, 0.0)
    meta[:, 0:LANES] = bits
    meta[:, LANES:] = flags
    ahead = jnp.where(
        iota((LANES, LANES), 0) < iota((LANES, LANES), 1),
        1.0,
        jnp.where(iota((LANES, LANES), 0) == iota((LANES, LANES), 1), 1000.0, 0.0),
    ).astype(BF16)
    places[...] = (dot(bits.astype(BF16), ahead) - 999.0).astype(jnp.int32)

    def clear(o, carry):
        for r in range(capacity):
            order_sm[o * capacity + r] = 0
        count_sm[o] = 0
        return carry

    lax.fori_loop(0, peers, clear, 0, unroll=8)

    def count(t, carry):
        o = owner_sm[t]
        r = count_sm[o]
        order_sm[o * capacity + r] = t
        count_sm[o] = r + 1
        return carry

    lax.fori_loop(0, tiles, count, 0, unroll=8)

    order = iota((packed + rest_ref.shape[1], LANES), 0)
    top_row = iota((packed, channels), 0) == 0
    group = peers // SENDS

    def send(i):
        part = pl.ds(i * group, group)
        return (
            pltpu.make_async_copy(packets.at[part], send_ref.at[part], send_sems.at[i]),
            pltpu.make_async_copy(rest.at[part], rest_ref.at[part], rest_sems.at[i]),
        )

    def pack(i, carry):
        for k in range(group):
            o = i * group + k
            held = [
                fluxes[pl.ds(pl.multiple_of(order_sm[o * capacity + r] * tile, tile), tile), :]
                for r in range(capacity)
            ]
            pick = jnp.where(order == places[pl.ds(o, 1), :], 1.0, 0.0).astype(BF16)
            packet = dot(pick[:, 0:pair], jnp.concatenate(held, axis=0))
            packets[o] = jnp.where(top_row, meta[pl.ds(o, 1), :], packet[0:packed]).astype(BF16)
            rest[o] = packet[packed:].astype(BF16)
        for copy in send(i):
            copy.start()
        return carry

    lax.fori_loop(0, SENDS, pack, 0)
    mark_ref[...] = jnp.zeros(mark_ref.shape, F32)
    for step in range(rows // block):
        leave(step).wait()
    for i in range(SENDS):
        for copy in send(i):
            copy.wait()


def atmosphere_step(
    mixed, own, top, bottom, conv_weight, gain, w_up, w_down, w_flux, owners, mask, peers, capacity, tile, packed
):
    rows, cols, channels = own.shape
    tiles = owners.shape[0]
    width = conv_weight.shape[0]
    margin = width // 2
    halves = channels // LANES
    hidden = w_up.shape[1]
    cells = rows * cols
    remaining = -(-(capacity * tile + 1 - packed) // 16) * 16
    return pl.pallas_call(
        functools.partial(atmosphere_kernel, tiles, capacity, tile),
        out_shape=[
            jax.ShapeDtypeStruct((rows, cols, channels), BF16),
            jax.ShapeDtypeStruct((peers, packed, channels), BF16),
            jax.ShapeDtypeStruct((peers, remaining, channels), BF16),
            jax.ShapeDtypeStruct((8, LANES), F32),
            pltpu.VMEM(mixed.shape, F32),
        ],
        in_specs=[IN_SMEM] + [IN_VMEM] * 11,
        out_specs=[ANY, ANY, ANY, IN_VMEM, IN_VMEM],
        input_output_aliases={1: 4},
        scratch_shapes=[
            pltpu.VMEM((halves, width * width, 8, LANES), F32),
            pltpu.VMEM((halves, margin, cols + 2 * RIM, LANES), F32),
            pltpu.VMEM((cells, channels), BF16),
            pltpu.SMEM((peers * capacity,), jnp.int32),
            pltpu.SMEM((peers,), jnp.int32),
            pltpu.VMEM((peers, 2 * LANES), F32),
            pltpu.VMEM((peers, LANES), jnp.int32),
            pltpu.VMEM((rows, cols, channels), BF16),
            pltpu.VMEM((peers, packed, channels), BF16),
            pltpu.VMEM((peers, remaining, channels), BF16),
            pltpu.SemaphoreType.DMA((rows,)),
            pltpu.SemaphoreType.DMA((SENDS,)),
            pltpu.SemaphoreType.DMA((SENDS,)),
        ],
        compiler_params=pltpu.CompilerParams(vmem_limit_bytes=VMEM_BYTES),
        cost_estimate=pl.CostEstimate(
            flops=2 * cells * channels * (2 * hidden + channels), bytes_accessed=12 * cells * channels,
            transcendentals=cells * hidden,
        ),
        name="atmosphere",
    )(
        owners, vmem(mixed), vmem(own), vmem(top), vmem(bottom), vmem(conv_weight), gain.reshape(1, -1), vmem(w_up),
        vmem(w_down), vmem(w_flux), owners.reshape(1, -1), mask,
    )


def fetch_kernel(mark_ref, *refs):
    count = (len(refs) - 1) // 2
    copies = [
        pltpu.make_async_copy(refs[i], refs[count + i], refs[-1].at[i]) for i in range(count)
    ]
    for copy in copies:
        copy.start()
    for copy in copies:
        copy.wait()


def fetch(mark, arrays):
    return pl.pallas_call(
        fetch_kernel,
        out_shape=[pltpu.VMEM(x.shape, x.dtype) for x in arrays],
        in_specs=[ANY] * (len(arrays) + 1),
        out_specs=[IN_VMEM] * len(arrays),
        scratch_shapes=[pltpu.SemaphoreType.DMA((len(arrays),))],
        compiler_params=pltpu.CompilerParams(vmem_limit_bytes=VMEM_BYTES),
        name="fetch",
    )(mark, *[hbm(x) for x in arrays])


def ocean_kernel(
    capacity, chain, state_ref, packet_hbm, gain_ref, up_ref, down_ref, out_hbm, over_ref, packet_ref, out_ref,
    in_sems, out_sems,
):
    peers, pair, channels = state_ref.shape
    packed = packet_ref.shape[1]
    tile = pair // capacity
    chains = peers // chain

    pieces = in_sems.shape[0] // chains
    piece = chain // pieces

    def arrive(i):
        part = pl.ds(i * piece, piece)
        return pltpu.make_async_copy(packet_hbm.at[part], packet_ref.at[part], in_sems.at[i])

    def leave(i):
        part = pl.ds(i * piece, piece)
        return pltpu.make_async_copy(out_ref.at[part], out_hbm.at[part], out_sems.at[i])

    for i in range(chains * pieces):
        arrive(i).start()
    ahead = jnp.where(
        iota((pair, LANES), 1) < iota((pair, LANES), 0),
        1.0,
        jnp.where(iota((pair, LANES), 1) == iota((pair, LANES), 0), 1000.0, 0.0),
    ).astype(BF16)
    order = iota((pair, packed), 1)

    def mix(i, over):
        for j in range(pieces):
            arrive(i * pieces + j).wait()
        first = i * chain
        head = jnp.concatenate([packet_ref[first + g, 0:1, :] for g in range(chain)], axis=0)
        place = lax.dot_general(
            ahead, head[:, 0:LANES], (((1,), (1,)), ((), ())), preferred_element_type=F32
        )
        place = (place - 999.0).astype(jnp.int32)
        flags = head[:, LANES:].astype(F32)
        states = []
        for g in range(chain):
            pick = jnp.where(order == place[:, g : g + 1], 1.0, 0.0).astype(BF16)
            states.append(state_ref[first + g].astype(F32) + dot(pick, packet_ref[first + g]))
        states = jnp.concatenate(states, axis=0)
        result = states + mixer(normalize(states, gain_ref[...]), up_ref, down_ref)
        for g in range(chain):
            for r in range(capacity):
                used = flags[g : g + 1, r : r + 1] > 0.0
                at = g * pair + r * tile
                part = jnp.where(used, result[at : at + tile], 0.0)
                out_ref[first + g, r * tile : (r + 1) * tile, :] = part.astype(BF16)
            if (g + 1) % piece == 0:
                leave(i * pieces + g // piece).start()
        return jnp.maximum(over, jnp.max(flags[:, capacity : capacity + 1], axis=0, keepdims=True))

    over = lax.fori_loop(0, chains, mix, jnp.zeros((1, 1), F32))
    over_ref[0, 0] = jnp.max(over)
    for i in range(chains * pieces):
        leave(i).wait()


def ocean_step(state, packets, gain, w_up, w_down, capacity):
    peers, pair, channels = state.shape
    packed = packets.shape[1]
    hidden = w_up.shape[1]
    chain = min(peers, 4096 // pair)
    cells = peers * pair
    return pl.pallas_call(
        functools.partial(ocean_kernel, capacity, chain),
        out_shape=[
            jax.ShapeDtypeStruct((peers, pair, channels), BF16),
            jax.ShapeDtypeStruct((1, 1), F32),
        ],
        in_specs=[IN_VMEM, ANY, IN_VMEM, IN_VMEM, IN_VMEM],
        out_specs=[ANY, IN_SMEM],
        scratch_shapes=[
            pltpu.VMEM((peers, packed, channels), BF16),
            pltpu.VMEM((peers, pair, channels), BF16),
            pltpu.SemaphoreType.DMA((8,)),
            pltpu.SemaphoreType.DMA((8,)),
        ],
        compiler_params=pltpu.CompilerParams(vmem_limit_bytes=VMEM_BYTES),
        cost_estimate=pl.CostEstimate(
            flops=4 * cells * channels * hidden, bytes_accessed=6 * cells * channels, transcendentals=cells * hidden
        ),
        name="ocean",
    )(vmem(state), hbm(packets), gain, vmem(w_up), vmem(w_down))


def per_device(
    atmosphere,
    conv_weight,
    atm_gain,
    atm_up,
    atm_down,
    flux_weight,
    land_mask,
    tile_owner,
    ocean_state,
    ocn_gain,
    ocn_up,
    ocn_down,
):
    margin = conv_weight.shape[0] // 2
    channels = atmosphere.shape[2]
    _, peers, capacity, tile, _ = ocean_state.shape
    pair = capacity * tile
    packed = -(-(pair * 13 // 16) // 8) * 8
    n_lon, n_lat = lax.axis_size("lon"), lax.axis_size("lat")
    owners = tile_owner.reshape(-1)
    state = ocean_state.reshape(peers, pair, channels)

    around = [(i, (i + 1) % n_lon) for i in range(n_lon)]
    own, conv_weight, first, last = edges(atmosphere, conv_weight)
    left = lax.ppermute(last, "lon", around)
    right = lax.ppermute(first, "lon", [(j, i) for i, j in around])
    mixed, products = conv_inner(own, conv_weight)
    up, down = widen(own, left, right, mixed, margin)
    north = [(i, i + 1) for i in range(n_lat - 1)]
    top = lax.ppermute(down, "lat", north)
    bottom = lax.ppermute(up, "lat", [(j, i) for i, j in north])
    mixed, w_up, w_down, w_flux = conv_outer(
        mixed, own, left, right, products, (atm_up, atm_down, flux_weight)
    )
    atm_out, packets, rest, mark, _ = atmosphere_step(
        mixed, own, top, bottom, conv_weight, atm_gain, w_up, w_down, w_flux, owners,
        land_mask.reshape(owners.shape[0], tile), peers, capacity, tile, packed,
    )

    def exchange(x):
        return lax.all_to_all(x, ("lat", "lon"), split_axis=0, concat_axis=0, tiled=True)

    arrived = exchange(packets)
    near = fetch(mark, (state, ocn_gain.reshape(1, -1), ocn_up, ocn_down))
    ocean_out, over = ocean_step(near[0], arrived, *near[1:], capacity)

    def with_rest(packed_out):
        everything = jnp.concatenate([arrived, exchange(rest)], axis=1)
        return ocean_step(near[0], everything, *near[1:], capacity)[0]

    ocean_out = lax.cond(over[0, 0] > 0, with_rest, lambda packed_out: packed_out, ocean_out)
    return atm_out, ocean_out.reshape(ocean_state.shape)


def solution(mesh):
    placed = (
        P("lat", "lon", None),
        P(),
        P(),
        P(),
        P(),
        P(),
        P("lat", "lon"),
        P("lat", "lon", None),
        P(("lat", "lon"), None, None, None, None),
        P(),
        P(),
        P(),
    )
    return jax.shard_map(
        per_device,
        mesh=mesh,
        in_specs=placed,
        out_specs=(P("lat", "lon", None), P(("lat", "lon"), None, None, None, None)),
        check_vma=False,
    )
```

```python
import functools

import jax
import jax.numpy as jnp
from jax import lax
from jax.experimental import pallas as pl
from jax.experimental.pallas import tpu as pltpu
from jax.sharding import PartitionSpec as P

LANES = 128
SENDS = 2
RIM = 8
SIDE = 16
VMEM_BYTES = 48 << 20
F32, BF16 = jnp.float32, jnp.bfloat16
ANY = pl.BlockSpec(memory_space=pl.ANY)
IN_VMEM = pl.BlockSpec(memory_space=pltpu.VMEM)
IN_SMEM = pl.BlockSpec(memory_space=pltpu.SMEM)


def hbm(x):
    return pltpu.with_memory_space_constraint(x, pltpu.HBM)


def vmem(x):
    return pltpu.with_memory_space_constraint(x, pltpu.VMEM)


def dot(a, b):
    return jnp.dot(a, b, preferred_element_type=F32)


def iota(shape, dim):
    return lax.broadcasted_iota(jnp.int32, shape, dim)


def spread_weights(w_ref, wb, width):
    for h in range(wb.shape[0]):
        for p in range(width):
            for q in range(width):
                row = w_ref[p, q : q + 1, h * LANES : (h + 1) * LANES]
                wb[h, p * width + q] = jnp.broadcast_to(row, (8, LANES))


PRODUCTS = (
    ((0,), (4,)),
    ((1,), (5,)),
    ((0, 1), (4, 5)),
    ((0, 2), (4, 6)),
    ((1, 3), (5,)),
    ((0, 1, 2, 3), (4, 5, 6)),
    ((2,), (6,)),
    ((3,),),
    ((2, 3), (6,)),
)
WIDTH = 7
MARGIN = WIDTH // 2
TAPS = sum(len(p) for p in PRODUCTS)


def spread_products(w_ref, wb):
    for h in range(wb.shape[0]):
        at = 0
        for product in PRODUCTS:
            for q in range(WIDTH):
                for tap in product:
                    row = None
                    for p in tap:
                        one = w_ref[p, q : q + 1, h * LANES : (h + 1) * LANES]
                        row = one if row is None else row + one
                    wb[h, at] = jnp.broadcast_to(row, (8, LANES))
                    at += 1


def combine_rows(get, put, rows):
    blank = jnp.zeros_like(get(0))
    seen = {}

    def row(r):
        if r < 0 or r >= rows:
            return blank
        if r not in seen:
            seen[r] = get(r)
        return seen[r]

    for m in range(rows // 4 + 1):
        x = [row(4 * m + a - MARGIN) for a in range(WIDTH)]
        d0, d1, d2 = x[0] - x[2], x[1] - x[3], x[2] - x[4]
        e1, e2 = x[5] - x[3], x[6] - x[4]
        values = (d0 - d1, d2 - d1, d1, x[2] - x[3], x[4] - x[3], x[3], -d2 - e1, e2 - e1, e1)
        for k, value in enumerate(values):
            put(k, m, value)


GIVES = ((0,), (1,), (0, 1), (0, 2), (1, 3), (0, 1, 2, 3), (2,), (3,), (2, 3))


def filter_rows(read, wb, h, count):
    out = [None] * (4 * count)
    at = 0
    for k, product in enumerate(PRODUCTS):
        acc = [None] * count
        for q in range(WIDTH):
            window = [read(k, m, q) for m in range(count + len(product) - 1)]
            for t in range(len(product)):
                w = wb[h, at]
                at += 1
                for m in range(count):
                    term = window[m + t] * w
                    acc[m] = term if acc[m] is None else acc[m] + term
        for m in range(count):
            for i in GIVES[k]:
                before = out[4 * m + i]
                out[4 * m + i] = acc[m] if before is None else before + acc[m]
    return out


def edges_kernel(x_ref, w_ref, own_ref, kept_ref, first_ref, last_ref, sems):
    cols = own_ref.shape[1]
    copies = [
        pltpu.make_async_copy(x_ref, own_ref, sems.at[0]),
        pltpu.make_async_copy(w_ref, kept_ref, sems.at[1]),
    ]
    for copy in copies:
        copy.start()
    for copy in copies:
        copy.wait()
    first_ref[...] = own_ref[:, 0:RIM]
    last_ref[...] = own_ref[:, cols - RIM :]


def edges(atmosphere, conv_weight):
    rows, _, channels = atmosphere.shape
    return pl.pallas_call(
        edges_kernel,
        out_shape=[
            pltpu.VMEM(atmosphere.shape, BF16),
            pltpu.VMEM(conv_weight.shape, F32),
            pltpu.VMEM((rows, RIM, channels), BF16),
            pltpu.VMEM((rows, RIM, channels), BF16),
        ],
        in_specs=[ANY, ANY],
        out_specs=[IN_VMEM] * 4,
        scratch_shapes=[pltpu.SemaphoreType.DMA((2,))],
        compiler_params=pltpu.CompilerParams(vmem_limit_bytes=VMEM_BYTES),
        name="edges",
    )(hbm(atmosphere), hbm(conv_weight))


GROUP = 8


def inner_kernel(own_ref, w_ref, mixed_ref, wb, xs, fs):
    rows, cols, channels = own_ref.shape
    spread_products(w_ref, wb)
    halves = channels // LANES
    first = SIDE - RIM
    each = (cols - 2 * SIDE) // 8
    for h in range(halves):
        xs[h] = own_ref[:, first : cols - first, h * LANES : (h + 1) * LANES].astype(F32)

    def prepare(t, carry):
        for h in range(halves):

            def put(k, m, value):
                fs[h, k, m, t] = value

            combine_rows(lambda r: xs[h, r, pl.ds(RIM - MARGIN + t, 8, stride=each)], put, rows)
        return carry

    lax.fori_loop(0, each + 2 * MARGIN, prepare, 0)

    def body(step, carry):
        m0 = (step // each) * GROUP
        t = step % each
        for h in range(halves):
            out = filter_rows(lambda k, m, q: fs[h, k, m0 + m, t + q], wb, h, GROUP)
            for i, value in enumerate(out):
                mixed_ref[h, m0 * 4 + i, pl.ds(SIDE + t, 8, stride=each)] = value
        return carry

    lax.fori_loop(0, (rows // 4 // GROUP) * each, body, 0)


def conv_inner(own, conv_weight):
    rows, cols, channels = own.shape
    halves = channels // LANES
    return pl.pallas_call(
        inner_kernel,
        out_shape=[
            pltpu.VMEM((halves, rows, cols, LANES), F32),
            pltpu.VMEM((halves, WIDTH * TAPS, 8, LANES), F32),
        ],
        in_specs=[IN_VMEM, IN_VMEM],
        out_specs=[IN_VMEM, IN_VMEM],
        scratch_shapes=[
            pltpu.VMEM((halves, rows, cols - 2 * (SIDE - RIM), LANES), F32),
            pltpu.VMEM((halves, len(PRODUCTS), rows // 4 + 1, (cols - 2 * SIDE) // 8 + 2 * MARGIN, 8, LANES), F32),
        ],
        compiler_params=pltpu.CompilerParams(vmem_limit_bytes=VMEM_BYTES),
        cost_estimate=pl.CostEstimate(
            flops=2 * rows * cols * channels * WIDTH * WIDTH, bytes_accessed=6 * rows * cols * channels, transcendentals=0
        ),
        name="conv_inner",
    )(vmem(own), vmem(conv_weight))


def outer_kernel(mixed_in, own_ref, left_ref, right_ref, wb, *refs, count):
    far, mixed_ref, near = refs[:count], refs[count], refs[count + 1 : 2 * count + 1]
    fs, sems = refs[2 * count + 1 :]
    fetches = [pltpu.make_async_copy(f, n, sems.at[i]) for i, (f, n) in enumerate(zip(far, near))]
    for fetch in fetches:
        fetch.start()
    rows, cols, channels = own_ref.shape
    halves = channels // LANES
    blocks = SIDE // 8
    for side in range(2):
        rim, edge = (left_ref, 0) if side == 0 else (right_ref, SIDE + RIM)
        body_at, own_at = (RIM, 0) if side == 0 else (0, cols - SIDE - RIM)
        for h in range(halves):
            part = slice(h * LANES, (h + 1) * LANES)

            def put_rim(k, m, value):
                fs[k, m, edge : edge + RIM] = value

            combine_rows(lambda r: rim[r, :, part].astype(F32), put_rim, rows)

            def prepare(c, carry):
                c0 = pl.multiple_of(c * 8, 8)

                def put(k, m, value):
                    fs[k, m, pl.ds(c0 + body_at, 8)] = value

                combine_rows(lambda r: own_ref[r, pl.ds(c0 + own_at, 8), part].astype(F32), put, rows)
                return carry

            lax.fori_loop(0, blocks + 1, prepare, 0)

            def body(step, carry):
                m0 = (step // blocks) * GROUP
                c0 = pl.multiple_of((step % blocks) * 8, 8)
                out = filter_rows(
                    lambda k, m, q: fs[k, m0 + m, pl.ds(c0 + (RIM - MARGIN + q), 8)], wb, h, GROUP
                )
                for i, value in enumerate(out):
                    mixed_ref[h, m0 * 4 + i, pl.ds(c0 + side * (cols - SIDE), 8)] = value
                return carry

            lax.fori_loop(0, (rows // 4 // GROUP) * blocks, body, 0)
    for fetch in fetches:
        fetch.wait()


def conv_outer(mixed, own, left, right, products, weights):
    rows, cols, channels = own.shape
    halves = channels // LANES
    count = len(weights)
    return pl.pallas_call(
        functools.partial(outer_kernel, count=count),
        out_shape=[pltpu.VMEM(mixed.shape, F32)] + [pltpu.VMEM(w.shape, w.dtype) for w in weights],
        in_specs=[IN_VMEM] * 5 + [ANY] * count,
        out_specs=[IN_VMEM] * (count + 1),
        input_output_aliases={0: 0},
        scratch_shapes=[
            pltpu.VMEM((len(PRODUCTS), rows // 4 + 1, SIDE + 2 * RIM, LANES), F32),
            pltpu.SemaphoreType.DMA((count,)),
        ],
        compiler_params=pltpu.CompilerParams(vmem_limit_bytes=VMEM_BYTES),
        cost_estimate=pl.CostEstimate(
            flops=4 * rows * RIM * channels * WIDTH * WIDTH, bytes_accessed=12 * rows * RIM * channels, transcendentals=0
        ),
        name="conv_outer",
    )(vmem(mixed), vmem(own), vmem(left), vmem(right), vmem(products), *[hbm(w) for w in weights])


def even_latitude():
    return lax.rem(lax.axis_index("lat"), 2) == 0


def widen_kernel(own_ref, left_ref, right_ref, mixed_ref, even_ref, odd_ref):
    margin = even_ref.shape[0]
    rows, cols, _ = own_ref.shape
    last = jnp.where(even_latitude(), rows - margin, 0)
    for out, at in ((even_ref, last), (odd_ref, rows - margin - last)):
        part = pl.ds(at, margin)
        out[:, 0:RIM] = left_ref[part]
        out[:, RIM : RIM + cols] = own_ref[part]
        out[:, RIM + cols :] = right_ref[part]


def widen(own, left, right, mixed, margin):
    rows, cols, channels = own.shape
    return pl.pallas_call(
        widen_kernel,
        out_shape=[pltpu.VMEM((margin, cols + 2 * RIM, channels), BF16)] * 2,
        in_specs=[IN_VMEM] * 4,
        out_specs=[IN_VMEM] * 2,
        compiler_params=pltpu.CompilerParams(vmem_limit_bytes=VMEM_BYTES),
        name="widen_rows",
    )(vmem(own), vmem(left), vmem(right), vmem(mixed))


def normalize(values, gain):
    average = jnp.mean(values, axis=-1, keepdims=True)
    centred = values - average
    spread = jnp.mean(centred * centred, axis=-1, keepdims=True)
    return (centred * lax.rsqrt(spread + 1e-06) * gain).astype(BF16)


def mixer(normed, up_ref, down_ref, chunk=256):
    c0 = 0.7978845608028654
    c1 = c0 * 0.044715
    total = None
    for j in range(0, up_ref.shape[1], chunk):
        x = dot(normed, up_ref[:, j : j + chunk])
        gate = jnp.tanh(x * (c0 + c1 * (x * x)))
        hidden = (x + x * gate).astype(BF16)
        part = dot(hidden, down_ref[j : j + chunk, :])
        total = part if total is None else total + part
    return 0.5 * total


def atmosphere_kernel(
    tiles, capacity, tile, owner_sm, mixed_in, atm_ref, even_ref, odd_ref, w_ref, gain_ref, up_ref, down_ref,
    flux_ref, owner_ref, mask_ref, out_ref, send_ref, rest_ref, mark_ref, mixed_ref,
    wb, strip, fluxes, order_sm, count_sm, meta, places, new_out, packets, rest, out_sems, send_sems, rest_sems,
):
    rows, cols, channels = atm_ref.shape
    width = w_ref.shape[0]
    margin = width // 2
    halves = channels // LANES
    peers, packed, _ = send_ref.shape
    pair = capacity * tile

    def lanes(h):
        return slice(h * LANES, (h + 1) * LANES)

    spread_weights(w_ref, wb, width)

    even = even_latitude()

    def latitude(if_even, if_odd, pairs):
        for h in range(halves):
            rows_in = [ref[:, :, lanes(h)].astype(F32) for ref in (if_even, if_odd)]
            strip[h] = jnp.where(even, *rows_in)

        def body(c, carry):
            c0 = pl.multiple_of(c * 8, 8)
            for h in range(halves):
                for i, taps in pairs:
                    acc = mixed_ref[h, i, pl.ds(c0, 8)]
                    for row, p in taps:
                        for q in range(width):
                            acc += strip[h, row, pl.ds(c0 + (RIM - margin + q), 8)] * wb[h, p * width + q]
                    mixed_ref[h, i, pl.ds(c0, 8)] = acc
            return carry

        lax.fori_loop(0, cols // 8, body, 0)

    latitude(odd_ref, even_ref, [(i, [(i + p, p) for p in range(margin - i)]) for i in range(margin)])
    latitude(
        even_ref,
        odd_ref,
        [
            (rows - margin + i, [(i - e, width - 1 - e) for e in range(i + 1)])
            for i in range(margin)
        ],
    )

    block = rows
    cells = block * cols

    def leave(step):
        part = pl.ds(step * block, block)
        return pltpu.make_async_copy(new_out.at[part], out_ref.at[part], out_sems.at[step])

    def mix(step, carry):
        r0 = step * block
        parts = [mixed_ref[h, pl.ds(r0, block)].reshape(cells, LANES) for h in range(halves)]
        normed = normalize(jnp.concatenate(parts, axis=1), gain_ref[...])
        branch = mixer(normed, up_ref, down_ref)
        new = (atm_ref[pl.ds(r0, block)].reshape(cells, channels).astype(F32) + branch).astype(BF16)
        new_out[pl.ds(r0, block)] = new.reshape(block, cols, channels)
        leave(step).start()
        fluxes[pl.ds(pl.multiple_of(step * cells, cells), cells), :] = dot(new, flux_ref[...]).astype(BF16)
        return carry

    lax.fori_loop(0, rows // block, mix, 0)

    member = (owner_ref[...] == iota((peers, tiles), 0)).astype(F32)
    before = (iota((tiles, tiles), 0) < iota((tiles, tiles), 1)).astype(BF16)
    rank = dot(member.astype(BF16), before)
    bits = jnp.zeros((peers, LANES), F32)
    flags = jnp.zeros((peers, LANES), F32)
    lane = iota((peers, LANES), 1)
    for r in range(capacity):
        chosen = jnp.where(rank == float(r), member, 0.0)
        at = (iota((tile, LANES), 1) == iota((tile, LANES), 0) + r * tile).astype(BF16)
        shifted = dot(mask_ref[...].astype(F32).astype(BF16), at).astype(BF16)
        bits += dot(chosen.astype(BF16), shifted)
        flags += jnp.where(lane == r, jnp.sum(chosen, axis=1, keepdims=True), 0.0)
    over = jnp.max(jnp.sum(bits, axis=1, keepdims=True), axis=0, keepdims=True) > float(packed - 1)
    flags += jnp.where((lane == capacity) & over, 1.0, 0.0)
    meta[:, 0:LANES] = bits
    meta[:, LANES:] = flags
    ahead = jnp.where(
        iota((LANES, LANES), 0) < iota((LANES, LANES), 1),
        1.0,
        jnp.where(iota((LANES, LANES), 0) == iota((LANES, LANES), 1), 1000.0, 0.0),
    ).astype(BF16)
    places[...] = (dot(bits.astype(BF16), ahead) - 999.0).astype(jnp.int32)

    def clear(o, carry):
        for r in range(capacity):
            order_sm[o * capacity + r] = 0
        count_sm[o] = 0
        return carry

    lax.fori_loop(0, peers, clear, 0, unroll=8)

    def count(t, carry):
        o = owner_sm[t]
        r = count_sm[o]
        order_sm[o * capacity + r] = t
        count_sm[o] = r + 1
        return carry

    lax.fori_loop(0, tiles, count, 0, unroll=8)

    order = iota((packed + rest_ref.shape[1], LANES), 0)
    top_row = iota((packed, channels), 0) == 0
    group = peers // SENDS

    def send(i):
        part = pl.ds(i * group, group)
        return (
            pltpu.make_async_copy(packets.at[part], send_ref.at[part], send_sems.at[i]),
            pltpu.make_async_copy(rest.at[part], rest_ref.at[part], rest_sems.at[i]),
        )

    def pack(i, carry):
        for k in range(group):
            o = i * group + k
            held = [
                fluxes[pl.ds(pl.multiple_of(order_sm[o * capacity + r] * tile, tile), tile), :]
                for r in range(capacity)
            ]
            pick = jnp.where(order == places[pl.ds(o, 1), :], 1.0, 0.0).astype(BF16)
            packet = dot(pick[:, 0:pair], jnp.concatenate(held, axis=0))
            packets[o] = jnp.where(top_row, meta[pl.ds(o, 1), :], packet[0:packed]).astype(BF16)
            rest[o] = packet[packed:].astype(BF16)
        for copy in send(i):
            copy.start()
        return carry

    lax.fori_loop(0, SENDS, pack, 0)
    mark_ref[...] = jnp.zeros(mark_ref.shape, F32)
    for step in range(rows // block):
        leave(step).wait()
    for i in range(SENDS):
        for copy in send(i):
            copy.wait()


def atmosphere_step(
    mixed, own, from_even, from_odd, conv_weight, gain, w_up, w_down, w_flux, owners, mask, peers, capacity, tile, packed
):
    rows, cols, channels = own.shape
    tiles = owners.shape[0]
    width = conv_weight.shape[0]
    margin = width // 2
    halves = channels // LANES
    hidden = w_up.shape[1]
    cells = rows * cols
    remaining = -(-(capacity * tile + 1 - packed) // 16) * 16
    return pl.pallas_call(
        functools.partial(atmosphere_kernel, tiles, capacity, tile),
        out_shape=[
            jax.ShapeDtypeStruct((rows, cols, channels), BF16),
            jax.ShapeDtypeStruct((peers, packed, channels), BF16),
            jax.ShapeDtypeStruct((peers, remaining, channels), BF16),
            jax.ShapeDtypeStruct((8, LANES), F32),
            pltpu.VMEM(mixed.shape, F32),
        ],
        in_specs=[IN_SMEM] + [IN_VMEM] * 11,
        out_specs=[ANY, ANY, ANY, IN_VMEM, IN_VMEM],
        input_output_aliases={1: 4},
        scratch_shapes=[
            pltpu.VMEM((halves, width * width, 8, LANES), F32),
            pltpu.VMEM((halves, margin, cols + 2 * RIM, LANES), F32),
            pltpu.VMEM((cells, channels), BF16),
            pltpu.SMEM((peers * capacity,), jnp.int32),
            pltpu.SMEM((peers,), jnp.int32),
            pltpu.VMEM((peers, 2 * LANES), F32),
            pltpu.VMEM((peers, LANES), jnp.int32),
            pltpu.VMEM((rows, cols, channels), BF16),
            pltpu.VMEM((peers, packed, channels), BF16),
            pltpu.VMEM((peers, remaining, channels), BF16),
            pltpu.SemaphoreType.DMA((rows,)),
            pltpu.SemaphoreType.DMA((SENDS,)),
            pltpu.SemaphoreType.DMA((SENDS,)),
        ],
        compiler_params=pltpu.CompilerParams(vmem_limit_bytes=VMEM_BYTES),
        cost_estimate=pl.CostEstimate(
            flops=2 * cells * channels * (2 * hidden + channels), bytes_accessed=12 * cells * channels,
            transcendentals=cells * hidden,
        ),
        name="atmosphere",
    )(
        owners, vmem(mixed), vmem(own), vmem(from_even), vmem(from_odd), vmem(conv_weight), gain.reshape(1, -1), vmem(w_up),
        vmem(w_down), vmem(w_flux), owners.reshape(1, -1), mask,
    )


def fetch_kernel(mark_ref, *refs):
    count = (len(refs) - 1) // 2
    copies = [
        pltpu.make_async_copy(refs[i], refs[count + i], refs[-1].at[i]) for i in range(count)
    ]
    for copy in copies:
        copy.start()
    for copy in copies:
        copy.wait()


def fetch(mark, arrays):
    return pl.pallas_call(
        fetch_kernel,
        out_shape=[pltpu.VMEM(x.shape, x.dtype) for x in arrays],
        in_specs=[ANY] * (len(arrays) + 1),
        out_specs=[IN_VMEM] * len(arrays),
        scratch_shapes=[pltpu.SemaphoreType.DMA((len(arrays),))],
        compiler_params=pltpu.CompilerParams(vmem_limit_bytes=VMEM_BYTES),
        name="fetch",
    )(mark, *[hbm(x) for x in arrays])


def ocean_kernel(
    capacity, chain, state_ref, packet_hbm, gain_ref, up_ref, down_ref, out_hbm, over_ref, packet_ref, out_ref,
    in_sems, out_sems,
):
    peers, pair, channels = state_ref.shape
    packed = packet_ref.shape[1]
    tile = pair // capacity
    chains = peers // chain

    pieces = in_sems.shape[0] // chains
    piece = chain // pieces

    def arrive(i):
        part = pl.ds(i * piece, piece)
        return pltpu.make_async_copy(packet_hbm.at[part], packet_ref.at[part], in_sems.at[i])

    def leave(i):
        part = pl.ds(i * piece, piece)
        return pltpu.make_async_copy(out_ref.at[part], out_hbm.at[part], out_sems.at[i])

    for i in range(chains * pieces):
        arrive(i).start()
    ahead = jnp.where(
        iota((pair, LANES), 1) < iota((pair, LANES), 0),
        1.0,
        jnp.where(iota((pair, LANES), 1) == iota((pair, LANES), 0), 1000.0, 0.0),
    ).astype(BF16)
    order = iota((pair, packed), 1).astype(F32).astype(BF16)

    def mix(i, over):
        for j in range(pieces):
            arrive(i * pieces + j).wait()
        first = i * chain
        head = jnp.concatenate([packet_ref[first + g, 0:1, :] for g in range(chain)], axis=0)
        place = lax.dot_general(
            ahead, head[:, 0:LANES], (((1,), (1,)), ((), ())), preferred_element_type=F32
        )
        place = (place - 999.0).astype(BF16)
        flags = head[:, LANES:].astype(F32)
        states = []
        for g in range(chain):
            pick = jnp.where(order == place[:, g : g + 1], jnp.ones_like(order), jnp.zeros_like(order))
            states.append(state_ref[first + g].astype(F32) + dot(pick, packet_ref[first + g]))
        states = jnp.concatenate(states, axis=0)
        result = states + mixer(normalize(states, gain_ref[...]), up_ref, down_ref)
        for g in range(chain):
            for r in range(capacity):
                used = flags[g : g + 1, r : r + 1] > 0.0
                at = g * pair + r * tile
                part = jnp.where(used, result[at : at + tile], 0.0)
                out_ref[first + g, r * tile : (r + 1) * tile, :] = part.astype(BF16)
            if (g + 1) % piece == 0:
                leave(i * pieces + g // piece).start()
        return jnp.maximum(over, jnp.max(flags[:, capacity : capacity + 1], axis=0, keepdims=True))

    over = lax.fori_loop(0, chains, mix, jnp.zeros((1, 1), F32))
    over_ref[0, 0] = jnp.max(over)
    for i in range(chains * pieces):
        leave(i).wait()


def ocean_step(state, packets, gain, w_up, w_down, capacity):
    peers, pair, channels = state.shape
    packed = packets.shape[1]
    hidden = w_up.shape[1]
    chain = min(peers, 4096 // pair)
    cells = peers * pair
    return pl.pallas_call(
        functools.partial(ocean_kernel, capacity, chain),
        out_shape=[
            jax.ShapeDtypeStruct((peers, pair, channels), BF16),
            jax.ShapeDtypeStruct((1, 1), F32),
        ],
        in_specs=[IN_VMEM, ANY, IN_VMEM, IN_VMEM, IN_VMEM],
        out_specs=[ANY, IN_SMEM],
        scratch_shapes=[
            pltpu.VMEM((peers, packed, channels), BF16),
            pltpu.VMEM((peers, pair, channels), BF16),
            pltpu.SemaphoreType.DMA((8,)),
            pltpu.SemaphoreType.DMA((8,)),
        ],
        compiler_params=pltpu.CompilerParams(vmem_limit_bytes=VMEM_BYTES),
        cost_estimate=pl.CostEstimate(
            flops=4 * cells * channels * hidden, bytes_accessed=6 * cells * channels, transcendentals=cells * hidden
        ),
        name="ocean",
    )(vmem(state), hbm(packets), gain, vmem(w_up), vmem(w_down))


def per_device(
    atmosphere,
    conv_weight,
    atm_gain,
    atm_up,
    atm_down,
    flux_weight,
    land_mask,
    tile_owner,
    ocean_state,
    ocn_gain,
    ocn_up,
    ocn_down,
):
    margin = conv_weight.shape[0] // 2
    channels = atmosphere.shape[2]
    _, peers, capacity, tile, _ = ocean_state.shape
    pair = capacity * tile
    packed = -(-(pair * 13 // 16) // 8) * 8
    n_lon, n_lat = lax.axis_size("lon"), lax.axis_size("lat")
    owners = tile_owner.reshape(-1)
    state = ocean_state.reshape(peers, pair, channels)

    around = [(i, (i + 1) % n_lon) for i in range(n_lon)]
    own, conv_weight, first, last = edges(atmosphere, conv_weight)
    left = lax.ppermute(last, "lon", around)
    right = lax.ppermute(first, "lon", [(j, i) for i, j in around])
    mixed, products = conv_inner(own, conv_weight)
    to_even, to_odd = widen(own, left, right, mixed, margin)

    def swap(x, first):
        pairs = [(i, i + 1) for i in range(first, n_lat - 1, 2)]
        return lax.ppermute(x, "lat", pairs + [(j, i) for i, j in pairs])

    from_even, from_odd = swap(to_even, 0), swap(to_odd, 1)
    mixed, w_up, w_down, w_flux = conv_outer(
        mixed, own, left, right, products, (atm_up, atm_down, flux_weight)
    )
    atm_out, packets, rest, mark, _ = atmosphere_step(
        mixed, own, from_even, from_odd, conv_weight, atm_gain, w_up, w_down, w_flux, owners,
        land_mask.reshape(owners.shape[0], tile), peers, capacity, tile, packed,
    )

    def exchange(x):
        return lax.all_to_all(x, ("lat", "lon"), split_axis=0, concat_axis=0, tiled=True)

    arrived = exchange(packets)
    near = fetch(mark, (state, ocn_gain.reshape(1, -1), ocn_up, ocn_down))
    ocean_out, over = ocean_step(near[0], arrived, *near[1:], capacity)

    def with_rest(packed_out):
        everything = jnp.concatenate([arrived, exchange(rest)], axis=1)
        return ocean_step(near[0], everything, *near[1:], capacity)[0]

    ocean_out = lax.cond(over[0, 0] > 0, with_rest, lambda packed_out: packed_out, ocean_out)
    return atm_out, ocean_out.reshape(ocean_state.shape)


def solution(mesh):
    placed = (
        P("lat", "lon", None),
        P(),
        P(),
        P(),
        P(),
        P(),
        P("lat", "lon"),
        P("lat", "lon", None),
        P(("lat", "lon"), None, None, None, None),
        P(),
        P(),
        P(),
    )
    return jax.shard_map(
        per_device,
        mesh=mesh,
        in_specs=placed,
        out_specs=(P("lat", "lon", None), P(("lat", "lon"), None, None, None, None)),
        check_vma=False,
    )
```

```python
import functools

import jax
import jax.numpy as jnp
from jax import lax
from jax.experimental import pallas as pl
from jax.experimental.pallas import tpu as pltpu
from jax.sharding import PartitionSpec as P

LANES = 128
SENDS = 2
RIM = 8
SIDE = 16
VMEM_BYTES = 48 << 20
F32, BF16 = jnp.float32, jnp.bfloat16
ANY = pl.BlockSpec(memory_space=pl.ANY)
IN_VMEM = pl.BlockSpec(memory_space=pltpu.VMEM)
IN_SMEM = pl.BlockSpec(memory_space=pltpu.SMEM)


def hbm(x):
    return pltpu.with_memory_space_constraint(x, pltpu.HBM)


def vmem(x):
    return pltpu.with_memory_space_constraint(x, pltpu.VMEM)


def dot(a, b):
    return jnp.dot(a, b, preferred_element_type=F32)


def iota(shape, dim):
    return lax.broadcasted_iota(jnp.int32, shape, dim)


def spread_weights(w_ref, wb, width):
    for h in range(wb.shape[0]):
        for p in range(width):
            for q in range(width):
                row = w_ref[p, q : q + 1, h * LANES : (h + 1) * LANES]
                wb[h, p * width + q] = jnp.broadcast_to(row, (8, LANES))


PRODUCTS = (
    ((0,), (4,)),
    ((1,), (5,)),
    ((0, 1), (4, 5)),
    ((0, 2), (4, 6)),
    ((1, 3), (5,)),
    ((0, 1, 2, 3), (4, 5, 6)),
    ((2,), (6,)),
    ((3,),),
    ((2, 3), (6,)),
)
WIDTH = 7
MARGIN = WIDTH // 2
TAPS = sum(len(p) for p in PRODUCTS)


def spread_products(w_ref, wb):
    for h in range(wb.shape[0]):
        at = 0
        for product in PRODUCTS:
            for q in range(WIDTH):
                for tap in product:
                    row = None
                    for p in tap:
                        one = w_ref[p, q : q + 1, h * LANES : (h + 1) * LANES]
                        row = one if row is None else row + one
                    wb[h, at] = jnp.broadcast_to(row, (8, LANES))
                    at += 1


def combine_rows(get, put, rows):
    blank = jnp.zeros_like(get(0))
    seen = {}

    def row(r):
        if r < 0 or r >= rows:
            return blank
        if r not in seen:
            seen[r] = get(r)
        return seen[r]

    for m in range(rows // 4 + 1):
        x = [row(4 * m + a - MARGIN) for a in range(WIDTH)]
        d0, d1, d2 = x[0] - x[2], x[1] - x[3], x[2] - x[4]
        e1, e2 = x[5] - x[3], x[6] - x[4]
        values = (d0 - d1, d2 - d1, d1, x[2] - x[3], x[4] - x[3], x[3], -d2 - e1, e2 - e1, e1)
        for k, value in enumerate(values):
            put(k, m, value)


GIVES = ((0,), (1,), (0, 1), (0, 2), (1, 3), (0, 1, 2, 3), (2,), (3,), (2, 3))


def filter_rows(read, wb, h, count):
    out = [None] * (4 * count)
    at = 0
    for k, product in enumerate(PRODUCTS):
        acc = [None] * count
        for q in range(WIDTH):
            window = [read(k, m, q) for m in range(count + len(product) - 1)]
            for t in range(len(product)):
                w = wb[h, at]
                at += 1
                for m in range(count):
                    term = window[m + t] * w
                    acc[m] = term if acc[m] is None else acc[m] + term
        for m in range(count):
            for i in GIVES[k]:
                before = out[4 * m + i]
                out[4 * m + i] = acc[m] if before is None else before + acc[m]
    return out


def even_band(axis):
    return lax.rem(lax.axis_index(axis), 2) == 0


def edges_kernel(x_ref, w_ref, own_ref, kept_ref, even_ref, odd_ref, sems):
    cols = own_ref.shape[1]
    copies = [
        pltpu.make_async_copy(x_ref, own_ref, sems.at[0]),
        pltpu.make_async_copy(w_ref, kept_ref, sems.at[1]),
    ]
    for copy in copies:
        copy.start()
    for copy in copies:
        copy.wait()
    even = even_band("lon")

    @pl.when(even)
    def _():
        even_ref[...] = own_ref[:, cols - RIM :]
        odd_ref[...] = own_ref[:, 0:RIM]

    @pl.when(jnp.logical_not(even))
    def _():
        even_ref[...] = own_ref[:, 0:RIM]
        odd_ref[...] = own_ref[:, cols - RIM :]


def edges(atmosphere, conv_weight):
    rows, _, channels = atmosphere.shape
    return pl.pallas_call(
        edges_kernel,
        out_shape=[
            pltpu.VMEM(atmosphere.shape, BF16),
            pltpu.VMEM(conv_weight.shape, F32),
            pltpu.VMEM((rows, RIM, channels), BF16),
            pltpu.VMEM((rows, RIM, channels), BF16),
        ],
        in_specs=[ANY, ANY],
        out_specs=[IN_VMEM] * 4,
        scratch_shapes=[pltpu.SemaphoreType.DMA((2,))],
        compiler_params=pltpu.CompilerParams(vmem_limit_bytes=VMEM_BYTES),
        name="edges",
    )(hbm(atmosphere), hbm(conv_weight))


GROUP = 8


def inner_kernel(own_ref, w_ref, mixed_ref, wb, xs, fs):
    rows, cols, channels = own_ref.shape
    spread_products(w_ref, wb)
    halves = channels // LANES
    first = SIDE - RIM
    each = (cols - 2 * SIDE) // 8
    for h in range(halves):
        xs[h] = own_ref[:, first : cols - first, h * LANES : (h + 1) * LANES].astype(F32)

    def prepare(t, carry):
        for h in range(halves):

            def put(k, m, value):
                fs[h, k, m, t] = value

            combine_rows(lambda r: xs[h, r, pl.ds(RIM - MARGIN + t, 8, stride=each)], put, rows)
        return carry

    lax.fori_loop(0, each + 2 * MARGIN, prepare, 0)

    def body(step, carry):
        m0 = (step // each) * GROUP
        t = step % each
        for h in range(halves):
            out = filter_rows(lambda k, m, q: fs[h, k, m0 + m, t + q], wb, h, GROUP)
            for i, value in enumerate(out):
                mixed_ref[h, m0 * 4 + i, pl.ds(SIDE + t, 8, stride=each)] = value
        return carry

    lax.fori_loop(0, (rows // 4 // GROUP) * each, body, 0)


def conv_inner(own, conv_weight):
    rows, cols, channels = own.shape
    halves = channels // LANES
    return pl.pallas_call(
        inner_kernel,
        out_shape=[
            pltpu.VMEM((halves, rows, cols, LANES), F32),
            pltpu.VMEM((halves, WIDTH * TAPS, 8, LANES), F32),
        ],
        in_specs=[IN_VMEM, IN_VMEM],
        out_specs=[IN_VMEM, IN_VMEM],
        scratch_shapes=[
            pltpu.VMEM((halves, rows, cols - 2 * (SIDE - RIM), LANES), F32),
            pltpu.VMEM((halves, len(PRODUCTS), rows // 4 + 1, (cols - 2 * SIDE) // 8 + 2 * MARGIN, 8, LANES), F32),
        ],
        compiler_params=pltpu.CompilerParams(vmem_limit_bytes=VMEM_BYTES),
        cost_estimate=pl.CostEstimate(
            flops=2 * rows * cols * channels * WIDTH * WIDTH, bytes_accessed=6 * rows * cols * channels, transcendentals=0
        ),
        name="conv_inner",
    )(vmem(own), vmem(conv_weight))


def outer_kernel(mixed_in, own_ref, even_ref, odd_ref, wb, *refs, count):
    far, mixed_ref, near = refs[:count], refs[count], refs[count + 1 : 2 * count + 1]
    fs, sems = refs[2 * count + 1 :]
    fetches = [pltpu.make_async_copy(f, n, sems.at[i]) for i, (f, n) in enumerate(zip(far, near))]
    for fetch in fetches:
        fetch.start()
    rows, cols, channels = own_ref.shape
    halves = channels // LANES
    blocks = SIDE // 8
    even = even_band("lon")
    for side in range(2):
        rims, edge = ((odd_ref, even_ref), 0) if side == 0 else ((even_ref, odd_ref), SIDE + RIM)
        body_at, own_at = (RIM, 0) if side == 0 else (0, cols - SIDE - RIM)
        for h in range(halves):
            part = slice(h * LANES, (h + 1) * LANES)

            def put_rim(k, m, value):
                fs[k, m, edge : edge + RIM] = value

            combine_rows(
                lambda r: jnp.where(even, *[rim[r, :, part].astype(F32) for rim in rims]), put_rim, rows
            )

            def prepare(c, carry):
                c0 = pl.multiple_of(c * 8, 8)

                def put(k, m, value):
                    fs[k, m, pl.ds(c0 + body_at, 8)] = value

                combine_rows(lambda r: own_ref[r, pl.ds(c0 + own_at, 8), part].astype(F32), put, rows)
                return carry

            lax.fori_loop(0, blocks + 1, prepare, 0)

            def body(step, carry):
                m0 = (step // blocks) * GROUP
                c0 = pl.multiple_of((step % blocks) * 8, 8)
                out = filter_rows(
                    lambda k, m, q: fs[k, m0 + m, pl.ds(c0 + (RIM - MARGIN + q), 8)], wb, h, GROUP
                )
                for i, value in enumerate(out):
                    mixed_ref[h, m0 * 4 + i, pl.ds(c0 + side * (cols - SIDE), 8)] = value
                return carry

            lax.fori_loop(0, (rows // 4 // GROUP) * blocks, body, 0)
    for fetch in fetches:
        fetch.wait()


def conv_outer(mixed, own, left, right, products, weights):
    rows, cols, channels = own.shape
    halves = channels // LANES
    count = len(weights)
    return pl.pallas_call(
        functools.partial(outer_kernel, count=count),
        out_shape=[pltpu.VMEM(mixed.shape, F32)] + [pltpu.VMEM(w.shape, w.dtype) for w in weights],
        in_specs=[IN_VMEM] * 5 + [ANY] * count,
        out_specs=[IN_VMEM] * (count + 1),
        input_output_aliases={0: 0},
        scratch_shapes=[
            pltpu.VMEM((len(PRODUCTS), rows // 4 + 1, SIDE + 2 * RIM, LANES), F32),
            pltpu.SemaphoreType.DMA((count,)),
        ],
        compiler_params=pltpu.CompilerParams(vmem_limit_bytes=VMEM_BYTES),
        cost_estimate=pl.CostEstimate(
            flops=4 * rows * RIM * channels * WIDTH * WIDTH, bytes_accessed=12 * rows * RIM * channels, transcendentals=0
        ),
        name="conv_outer",
    )(vmem(mixed), vmem(own), vmem(left), vmem(right), vmem(products), *[hbm(w) for w in weights])


def widen_kernel(own_ref, lon_even_ref, lon_odd_ref, mixed_ref, even_ref, odd_ref):
    margin = even_ref.shape[0]
    rows, cols, _ = own_ref.shape
    last = jnp.where(even_band("lat"), rows - margin, 0)
    for out, at in ((even_ref, last), (odd_ref, rows - margin - last)):
        part = pl.ds(at, margin)
        out[:, RIM : RIM + cols] = own_ref[part]

        @pl.when(even_band("lon"))
        def _(out=out, part=part):
            out[:, 0:RIM] = lon_odd_ref[part]
            out[:, RIM + cols :] = lon_even_ref[part]

        @pl.when(jnp.logical_not(even_band("lon")))
        def _(out=out, part=part):
            out[:, 0:RIM] = lon_even_ref[part]
            out[:, RIM + cols :] = lon_odd_ref[part]


def widen(own, left, right, mixed, margin):
    rows, cols, channels = own.shape
    return pl.pallas_call(
        widen_kernel,
        out_shape=[pltpu.VMEM((margin, cols + 2 * RIM, channels), BF16)] * 2,
        in_specs=[IN_VMEM] * 4,
        out_specs=[IN_VMEM] * 2,
        compiler_params=pltpu.CompilerParams(vmem_limit_bytes=VMEM_BYTES),
        name="widen_rows",
    )(vmem(own), vmem(left), vmem(right), vmem(mixed))


def normalize(values, gain):
    average = jnp.mean(values, axis=-1, keepdims=True)
    centred = values - average
    spread = jnp.mean(centred * centred, axis=-1, keepdims=True)
    return (centred * lax.rsqrt(spread + 1e-06) * gain).astype(BF16)


def mixer(normed, up_ref, down_ref, chunk=256):
    c0 = 0.7978845608028654
    c1 = c0 * 0.044715
    total = None
    for j in range(0, up_ref.shape[1], chunk):
        x = dot(normed, up_ref[:, j : j + chunk])
        gate = jnp.tanh(x * (c0 + c1 * (x * x)))
        hidden = (x + x * gate).astype(BF16)
        part = dot(hidden, down_ref[j : j + chunk, :])
        total = part if total is None else total + part
    return 0.5 * total


def atmosphere_kernel(
    tiles, capacity, tile, owner_sm, mixed_in, atm_ref, even_ref, odd_ref, w_ref, gain_ref, up_ref, down_ref,
    flux_ref, owner_ref, mask_ref, out_ref, send_ref, rest_ref, mark_ref, mixed_ref,
    wb, strip, fluxes, order_sm, count_sm, meta, places, new_out, packets, rest, out_sems, send_sems, rest_sems,
):
    rows, cols, channels = atm_ref.shape
    width = w_ref.shape[0]
    margin = width // 2
    halves = channels // LANES
    peers, packed, _ = send_ref.shape
    pair = capacity * tile

    def lanes(h):
        return slice(h * LANES, (h + 1) * LANES)

    spread_weights(w_ref, wb, width)

    even = even_band("lat")

    def latitude(if_even, if_odd, pairs):
        for h in range(halves):
            rows_in = [ref[:, :, lanes(h)].astype(F32) for ref in (if_even, if_odd)]
            strip[h] = jnp.where(even, *rows_in)

        def body(c, carry):
            c0 = pl.multiple_of(c * 8, 8)
            for h in range(halves):
                for i, taps in pairs:
                    acc = mixed_ref[h, i, pl.ds(c0, 8)]
                    for row, p in taps:
                        for q in range(width):
                            acc += strip[h, row, pl.ds(c0 + (RIM - margin + q), 8)] * wb[h, p * width + q]
                    mixed_ref[h, i, pl.ds(c0, 8)] = acc
            return carry

        lax.fori_loop(0, cols // 8, body, 0)

    latitude(odd_ref, even_ref, [(i, [(i + p, p) for p in range(margin - i)]) for i in range(margin)])
    latitude(
        even_ref,
        odd_ref,
        [
            (rows - margin + i, [(i - e, width - 1 - e) for e in range(i + 1)])
            for i in range(margin)
        ],
    )

    block = rows
    cells = block * cols

    def leave(step):
        part = pl.ds(step * block, block)
        return pltpu.make_async_copy(new_out.at[part], out_ref.at[part], out_sems.at[step])

    def mix(step, carry):
        r0 = step * block
        parts = [mixed_ref[h, pl.ds(r0, block)].reshape(cells, LANES) for h in range(halves)]
        normed = normalize(jnp.concatenate(parts, axis=1), gain_ref[...])
        branch = mixer(normed, up_ref, down_ref)
        new = (atm_ref[pl.ds(r0, block)].reshape(cells, channels).astype(F32) + branch).astype(BF16)
        new_out[pl.ds(r0, block)] = new.reshape(block, cols, channels)
        leave(step).start()
        fluxes[pl.ds(pl.multiple_of(step * cells, cells), cells), :] = dot(new, flux_ref[...]).astype(BF16)
        return carry

    lax.fori_loop(0, rows // block, mix, 0)

    member = (owner_ref[...] == iota((peers, tiles), 0)).astype(F32)
    before = (iota((tiles, tiles), 0) < iota((tiles, tiles), 1)).astype(BF16)
    rank = dot(member.astype(BF16), before)
    bits = jnp.zeros((peers, LANES), F32)
    flags = jnp.zeros((peers, LANES), F32)
    lane = iota((peers, LANES), 1)
    for r in range(capacity):
        chosen = jnp.where(rank == float(r), member, 0.0)
        at = (iota((tile, LANES), 1) == iota((tile, LANES), 0) + r * tile).astype(BF16)
        shifted = dot(mask_ref[...].astype(F32).astype(BF16), at).astype(BF16)
        bits += dot(chosen.astype(BF16), shifted)
        flags += jnp.where(lane == r, jnp.sum(chosen, axis=1, keepdims=True), 0.0)
    over = jnp.max(jnp.sum(bits, axis=1, keepdims=True), axis=0, keepdims=True) > float(packed - 1)
    flags += jnp.where((lane == capacity) & over, 1.0, 0.0)
    meta[:, 0:LANES] = bits
    meta[:, LANES:] = flags
    ahead = jnp.where(
        iota((LANES, LANES), 0) < iota((LANES, LANES), 1),
        1.0,
        jnp.where(iota((LANES, LANES), 0) == iota((LANES, LANES), 1), 1000.0, 0.0),
    ).astype(BF16)
    places[...] = (dot(bits.astype(BF16), ahead) - 999.0).astype(jnp.int32)

    def clear(o, carry):
        for r in range(capacity):
            order_sm[o * capacity + r] = 0
        count_sm[o] = 0
        return carry

    lax.fori_loop(0, peers, clear, 0, unroll=8)

    def count(t, carry):
        o = owner_sm[t]
        r = count_sm[o]
        order_sm[o * capacity + r] = t
        count_sm[o] = r + 1
        return carry

    lax.fori_loop(0, tiles, count, 0, unroll=8)

    order = iota((packed + rest_ref.shape[1], LANES), 0)
    top_row = iota((packed, channels), 0) == 0
    group = peers // SENDS

    def send(i):
        part = pl.ds(i * group, group)
        return (
            pltpu.make_async_copy(packets.at[part], send_ref.at[part], send_sems.at[i]),
            pltpu.make_async_copy(rest.at[part], rest_ref.at[part], rest_sems.at[i]),
        )

    def pack(i, carry):
        for k in range(group):
            o = i * group + k
            held = [
                fluxes[pl.ds(pl.multiple_of(order_sm[o * capacity + r] * tile, tile), tile), :]
                for r in range(capacity)
            ]
            pick = jnp.where(order == places[pl.ds(o, 1), :], 1.0, 0.0).astype(BF16)
            packet = dot(pick[:, 0:pair], jnp.concatenate(held, axis=0))
            packets[o] = jnp.where(top_row, meta[pl.ds(o, 1), :], packet[0:packed]).astype(BF16)
            rest[o] = packet[packed:].astype(BF16)
        for copy in send(i):
            copy.start()
        return carry

    lax.fori_loop(0, SENDS, pack, 0)
    mark_ref[...] = jnp.zeros(mark_ref.shape, F32)
    for step in range(rows // block):
        leave(step).wait()
    for i in range(SENDS):
        for copy in send(i):
            copy.wait()


def atmosphere_step(
    mixed, own, from_even, from_odd, conv_weight, gain, w_up, w_down, w_flux, owners, mask, peers, capacity, tile, packed
):
    rows, cols, channels = own.shape
    tiles = owners.shape[0]
    width = conv_weight.shape[0]
    margin = width // 2
    halves = channels // LANES
    hidden = w_up.shape[1]
    cells = rows * cols
    remaining = -(-(capacity * tile + 1 - packed) // 16) * 16
    return pl.pallas_call(
        functools.partial(atmosphere_kernel, tiles, capacity, tile),
        out_shape=[
            jax.ShapeDtypeStruct((rows, cols, channels), BF16),
            jax.ShapeDtypeStruct((peers, packed, channels), BF16),
            jax.ShapeDtypeStruct((peers, remaining, channels), BF16),
            jax.ShapeDtypeStruct((8, LANES), F32),
            pltpu.VMEM(mixed.shape, F32),
        ],
        in_specs=[IN_SMEM] + [IN_VMEM] * 11,
        out_specs=[ANY, ANY, ANY, IN_VMEM, IN_VMEM],
        input_output_aliases={1: 4},
        scratch_shapes=[
            pltpu.VMEM((halves, width * width, 8, LANES), F32),
            pltpu.VMEM((halves, margin, cols + 2 * RIM, LANES), F32),
            pltpu.VMEM((cells, channels), BF16),
            pltpu.SMEM((peers * capacity,), jnp.int32),
            pltpu.SMEM((peers,), jnp.int32),
            pltpu.VMEM((peers, 2 * LANES), F32),
            pltpu.VMEM((peers, LANES), jnp.int32),
            pltpu.VMEM((rows, cols, channels), BF16),
            pltpu.VMEM((peers, packed, channels), BF16),
            pltpu.VMEM((peers, remaining, channels), BF16),
            pltpu.SemaphoreType.DMA((rows,)),
            pltpu.SemaphoreType.DMA((SENDS,)),
            pltpu.SemaphoreType.DMA((SENDS,)),
        ],
        compiler_params=pltpu.CompilerParams(vmem_limit_bytes=VMEM_BYTES),
        cost_estimate=pl.CostEstimate(
            flops=2 * cells * channels * (2 * hidden + channels), bytes_accessed=12 * cells * channels,
            transcendentals=cells * hidden,
        ),
        name="atmosphere",
    )(
        owners, vmem(mixed), vmem(own), vmem(from_even), vmem(from_odd), vmem(conv_weight), gain.reshape(1, -1), vmem(w_up),
        vmem(w_down), vmem(w_flux), owners.reshape(1, -1), mask,
    )


def fetch_kernel(mark_ref, *refs):
    count = (len(refs) - 1) // 2
    copies = [
        pltpu.make_async_copy(refs[i], refs[count + i], refs[-1].at[i]) for i in range(count)
    ]
    for copy in copies:
        copy.start()
    for copy in copies:
        copy.wait()


def fetch(mark, arrays):
    return pl.pallas_call(
        fetch_kernel,
        out_shape=[pltpu.VMEM(x.shape, x.dtype) for x in arrays],
        in_specs=[ANY] * (len(arrays) + 1),
        out_specs=[IN_VMEM] * len(arrays),
        scratch_shapes=[pltpu.SemaphoreType.DMA((len(arrays),))],
        compiler_params=pltpu.CompilerParams(vmem_limit_bytes=VMEM_BYTES),
        name="fetch",
    )(mark, *[hbm(x) for x in arrays])


def ocean_kernel(
    capacity, chain, state_ref, packet_hbm, gain_ref, up_ref, down_ref, out_hbm, over_ref, packet_ref, out_ref,
    in_sems, out_sems,
):
    peers, pair, channels = state_ref.shape
    packed = packet_ref.shape[1]
    tile = pair // capacity
    chains = peers // chain

    pieces = in_sems.shape[0] // chains
    piece = chain // pieces

    def arrive(i):
        part = pl.ds(i * piece, piece)
        return pltpu.make_async_copy(packet_hbm.at[part], packet_ref.at[part], in_sems.at[i])

    def leave(i):
        part = pl.ds(i * piece, piece)
        return pltpu.make_async_copy(out_ref.at[part], out_hbm.at[part], out_sems.at[i])

    for i in range(chains * pieces):
        arrive(i).start()
    ahead = jnp.where(
        iota((pair, LANES), 1) < iota((pair, LANES), 0),
        1.0,
        jnp.where(iota((pair, LANES), 1) == iota((pair, LANES), 0), 1000.0, 0.0),
    ).astype(BF16)
    order = iota((pair, packed), 1).astype(F32).astype(BF16)

    def mix(i, over):
        for j in range(pieces):
            arrive(i * pieces + j).wait()
        first = i * chain
        head = jnp.concatenate([packet_ref[first + g, 0:1, :] for g in range(chain)], axis=0)
        place = lax.dot_general(
            ahead, head[:, 0:LANES], (((1,), (1,)), ((), ())), preferred_element_type=F32
        )
        place = (place - 999.0).astype(BF16)
        flags = head[:, LANES:].astype(F32)
        states = []
        for g in range(chain):
            pick = jnp.where(order == place[:, g : g + 1], jnp.ones_like(order), jnp.zeros_like(order))
            states.append(state_ref[first + g].astype(F32) + dot(pick, packet_ref[first + g]))
        states = jnp.concatenate(states, axis=0)
        result = states + mixer(normalize(states, gain_ref[...]), up_ref, down_ref)
        for g in range(chain):
            for r in range(capacity):
                used = flags[g : g + 1, r : r + 1] > 0.0
                at = g * pair + r * tile
                part = jnp.where(used, result[at : at + tile], 0.0)
                out_ref[first + g, r * tile : (r + 1) * tile, :] = part.astype(BF16)
            if (g + 1) % piece == 0:
                leave(i * pieces + g // piece).start()
        return jnp.maximum(over, jnp.max(flags[:, capacity : capacity + 1], axis=0, keepdims=True))

    over = lax.fori_loop(0, chains, mix, jnp.zeros((1, 1), F32))
    over_ref[0, 0] = jnp.max(over)
    for i in range(chains * pieces):
        leave(i).wait()


def ocean_step(state, packets, gain, w_up, w_down, capacity):
    peers, pair, channels = state.shape
    packed = packets.shape[1]
    hidden = w_up.shape[1]
    chain = min(peers, 4096 // pair)
    cells = peers * pair
    return pl.pallas_call(
        functools.partial(ocean_kernel, capacity, chain),
        out_shape=[
            jax.ShapeDtypeStruct((peers, pair, channels), BF16),
            jax.ShapeDtypeStruct((1, 1), F32),
        ],
        in_specs=[IN_VMEM, ANY, IN_VMEM, IN_VMEM, IN_VMEM],
        out_specs=[ANY, IN_SMEM],
        scratch_shapes=[
            pltpu.VMEM((peers, packed, channels), BF16),
            pltpu.VMEM((peers, pair, channels), BF16),
            pltpu.SemaphoreType.DMA((8,)),
            pltpu.SemaphoreType.DMA((8,)),
        ],
        compiler_params=pltpu.CompilerParams(vmem_limit_bytes=VMEM_BYTES),
        cost_estimate=pl.CostEstimate(
            flops=4 * cells * channels * hidden, bytes_accessed=6 * cells * channels, transcendentals=cells * hidden
        ),
        name="ocean",
    )(vmem(state), hbm(packets), gain, vmem(w_up), vmem(w_down))


def per_device(
    atmosphere,
    conv_weight,
    atm_gain,
    atm_up,
    atm_down,
    flux_weight,
    land_mask,
    tile_owner,
    ocean_state,
    ocn_gain,
    ocn_up,
    ocn_down,
):
    margin = conv_weight.shape[0] // 2
    channels = atmosphere.shape[2]
    _, peers, capacity, tile, _ = ocean_state.shape
    pair = capacity * tile
    packed = -(-(pair * 13 // 16) // 8) * 8
    n_lon, n_lat = lax.axis_size("lon"), lax.axis_size("lat")
    owners = tile_owner.reshape(-1)
    state = ocean_state.reshape(peers, pair, channels)

    own, conv_weight, lon_even, lon_odd = edges(atmosphere, conv_weight)

    def swap_around(x, first):
        pairs = [(i, (i + 1) % n_lon) for i in range(first, n_lon, 2)]
        return lax.ppermute(x, "lon", pairs + [(j, i) for i, j in pairs])

    lon_odd, lon_even = swap_around(lon_odd, 1), swap_around(lon_even, 0)
    mixed, products = conv_inner(own, conv_weight)
    to_even, to_odd = widen(own, lon_even, lon_odd, mixed, margin)

    def swap(x, first):
        pairs = [(i, i + 1) for i in range(first, n_lat - 1, 2)]
        return lax.ppermute(x, "lat", pairs + [(j, i) for i, j in pairs])

    from_even, from_odd = swap(to_even, 0), swap(to_odd, 1)
    mixed, w_up, w_down, w_flux = conv_outer(
        mixed, own, lon_even, lon_odd, products, (atm_up, atm_down, flux_weight)
    )
    atm_out, packets, rest, mark, _ = atmosphere_step(
        mixed, own, from_even, from_odd, conv_weight, atm_gain, w_up, w_down, w_flux, owners,
        land_mask.reshape(owners.shape[0], tile), peers, capacity, tile, packed,
    )

    def exchange(x):
        return lax.all_to_all(x, ("lat", "lon"), split_axis=0, concat_axis=0, tiled=True)

    arrived = exchange(packets)
    near = fetch(mark, (state, ocn_gain.reshape(1, -1), ocn_up, ocn_down))
    ocean_out, over = ocean_step(near[0], arrived, *near[1:], capacity)

    def with_rest(packed_out):
        everything = jnp.concatenate([arrived, exchange(rest)], axis=1)
        return ocean_step(near[0], everything, *near[1:], capacity)[0]

    ocean_out = lax.cond(over[0, 0] > 0, with_rest, lambda packed_out: packed_out, ocean_out)
    return atm_out, ocean_out.reshape(ocean_state.shape)


def solution(mesh):
    placed = (
        P("lat", "lon", None),
        P(),
        P(),
        P(),
        P(),
        P(),
        P("lat", "lon"),
        P("lat", "lon", None),
        P(("lat", "lon"), None, None, None, None),
        P(),
        P(),
        P(),
    )
    return jax.shard_map(
        per_device,
        mesh=mesh,
        in_specs=placed,
        out_specs=(P("lat", "lon", None), P(("lat", "lon"), None, None, None, None)),
        check_vma=False,
    )
```
